32 devices in a mesh: pre: 2 (over x), grp: 4 (over y, core), dec: 4 (over z).
Axes of the slice: x: 2, y: 2, z: 4, core: 2. Of those that a mesh axis runs over, the one named last changes fastest.
Arguments:
- prompt_queries: bfloat16 [16, 1024, 8192], P(('grp', 'dec'), None, 'pre'), may hold values from -6 to 6
- prompt_keys: bfloat16 [16, 1024, 8192], P(('grp', 'dec'), None, 'pre'), may hold values from -6 to 6
- prompt_values: bfloat16 [16, 1024, 8192], P(('grp', 'dec'), None, 'pre'), may hold values from -6 to 6
- prompt_decay: float32 [16, 64, 1024], P(('grp', 'dec'), 'pre'), may hold values from -1 to 0
- prompt_lengths: int32 [16], P(('grp', 'dec')), may hold values from 256 to 1024
- norm_gain: float32 [8192], P('pre'), may hold values from 0.1 to 1.9
- decode_owner: int32 [16], replicated, may hold values from 0 to 3, as said below
- parent_beam: int32 [16, 16], P('grp'), may hold values from 0 to 15, as said below
- step_queries: bfloat16 [2, 16, 16, 8192], P(None, 'grp', 'dec', 'pre'), may hold values from -6 to 6
- step_keys: bfloat16 [2, 16, 16, 8192], P(None, 'grp', 'dec', 'pre'), may hold values from -12 to 12
- step_values: bfloat16 [2, 16, 16, 8192], P(None, 'grp', 'dec', 'pre'), may hold values from -12 to 12
- step_decay: float32 [2, 16, 16, 64], P(None, 'grp', None, 'pre'), may hold values from -1 to -0.05
Outputs:
- prompt_out: bfloat16 [16, 1024, 8192], P(('grp', 'dec'), None, 'pre')
- step_out: bfloat16 [2, 16, 16, 8192], P(None, 'grp', 'dec', 'pre')
The draws below stay inside these ranges and needn't reach their ends.
Inputs may be any that keep to these rules, and one draw needn't show every extreme that they name: `decode_owner`: each value of grp owns exactly 4 prompts. Among the prompts of one index of dec (over all indices of grp), at most 2 have the same owner, and in every index of dec some owner has 2 of them. `parent_beam`: A parent is a beam of the same slot. In each slot, each block of 16 // 4 beams held by one index of dec has exactly one row whose parent lies in another block. Over the 4 slots of one index of grp, the rows of one block take parents from one other block at most 2 times, and this is reached.
All inputs are finite; a program needn't handle non-finite values.
Results may differ from the reference program's by a relative error of at most 0.0041.
Values may be sent and summed in bfloat16 or wider, within the bound.
No kernel may reach another device: no remote copies, remote signals or barrier semaphores. Data moves between devices by JAX's collectives and lax.ppermute only.
A program may use at most 256 MiB of HBM per device.

```python
import math
import jax
import jax.numpy as jnp
from jax import lax

HEAD_COUNT = 64
HD = 128
BEAMS = 16
BLK = 256
DSTEPS = 2
SEQ_DEV = 1
PROMPT_LENGTH = 1024
ATT = 8192
PROMPT_COUNT = 16
N_GRP = 4
N_DEC = 4


def draw_prompt_decay(key, part):
    key = jax.random.fold_in(key, 11)
    beam_flows = jax.random.split(key, 6)
    slow_share = 0.5
    slow_head = jax.random.uniform(beam_flows[0], (PROMPT_COUNT, HEAD_COUNT, 1)) < slow_share
    fast_rate = jnp.exp(jax.random.uniform(beam_flows[1], (PROMPT_COUNT, HEAD_COUNT, 1), minval=math.log(1.0 / 50.0), maxval=math.log(1.0 / 30.0)))
    slow_rate = jnp.exp(jax.random.uniform(beam_flows[2], (PROMPT_COUNT, HEAD_COUNT, 1), minval=math.log(0.02 / PROMPT_LENGTH), maxval=math.log(0.5 / PROMPT_LENGTH)))
    decay_rate = jnp.where(slow_head, slow_rate, fast_rate)
    rough_factor = jnp.exp(jax.random.uniform(beam_flows[3], (PROMPT_COUNT, HEAD_COUNT, PROMPT_LENGTH), minval=math.log(0.5), maxval=math.log(2.0)))
    surge_position = jax.random.randint(beam_flows[4], (PROMPT_COUNT, HEAD_COUNT, 2), 0, PROMPT_LENGTH)
    position_ids = jnp.arange(PROMPT_LENGTH)
    marked_rows = jnp.any(position_ids[None, None, :, None] == surge_position[:, :, None, :], axis=-1)
    kept_share = jax.random.uniform(beam_flows[5], (PROMPT_COUNT, HEAD_COUNT, PROMPT_LENGTH), minval=0.5, maxval=0.8)
    return (-decay_rate * rough_factor + jnp.where(marked_rows, jnp.log(kept_share), 0.0)).astype(jnp.float32)


def draw_prompt_lengths(key, part):
    key = jax.random.fold_in(key, 41)
    beam_flows = jax.random.split(key, 2)
    drawn = jax.random.randint(beam_flows[0], (PROMPT_COUNT,), PROMPT_LENGTH // 4, PROMPT_LENGTH + 1)
    longest = jax.random.randint(beam_flows[1], (), 0, PROMPT_COUNT)
    return jnp.where(jnp.arange(PROMPT_COUNT) == longest, PROMPT_LENGTH, drawn).astype(jnp.int32)


def draw_decode_owner(key, part):
    key = jax.random.fold_in(key, 23)
    beam_flows = jax.random.split(key, 4)
    half_count = N_DEC // 2
    column_order = jax.random.permutation(beam_flows[0], N_DEC)
    first_owner = jax.random.randint(beam_flows[1], (half_count,), 0, N_GRP)
    second_owner = (first_owner + jax.random.randint(beam_flows[2], (half_count,), 1, N_GRP)) % N_GRP
    owner_index = jnp.arange(N_GRP)
    plus_part = (owner_index[None, :] == first_owner[:, None]).astype(jnp.int32) - (owner_index[None, :] == second_owner[:, None]).astype(jnp.int32)
    deltas = jnp.concatenate([plus_part, -plus_part], axis=0)
    counts = jnp.zeros((N_DEC, N_GRP), jnp.int32).at[column_order].set(SEQ_DEV + deltas)
    bounds = jnp.cumsum(counts, axis=1)
    column_size = N_GRP * SEQ_DEV
    slot_index = jnp.arange(column_size)
    owner_list = jnp.sum((bounds[:, None, :] <= slot_index[None, :, None]).astype(jnp.int32), axis=-1)
    shuffles = jax.vmap(lambda sub_key: jax.random.permutation(sub_key, column_size))(jax.random.split(beam_flows[3], N_DEC))
    shuffled = jnp.take_along_axis(owner_list, shuffles, axis=1)
    return shuffled.reshape(N_DEC, N_GRP, SEQ_DEV).transpose(1, 0, 2).reshape(PROMPT_COUNT).astype(jnp.int32)


def draw_parent_beam(key, part):
    key = jax.random.fold_in(key, 37)
    beam_flows = jax.random.split(key, 4)
    per_block = BEAMS // N_DEC
    offset = jax.random.randint(beam_flows[0], (), 0, N_DEC - 1)
    slot_index = jnp.arange(PROMPT_COUNT)[:, None]
    block_index = jnp.arange(N_DEC)[None, :]
    source_block = (block_index + 1 + (slot_index + offset) % (N_DEC - 1)) % N_DEC
    crossing = jax.random.randint(beam_flows[1], (PROMPT_COUNT, N_DEC), 0, per_block)
    far_parent = source_block * per_block + jax.random.randint(beam_flows[2], (PROMPT_COUNT, N_DEC), 0, per_block)
    near_parent = block_index[:, :, None] * per_block + jax.random.randint(beam_flows[3], (PROMPT_COUNT, N_DEC, per_block), 0, per_block)
    within = jnp.arange(per_block)[None, None, :]
    chosen = jnp.where(within == crossing[:, :, None], far_parent[:, :, None], near_parent)
    return chosen.reshape(PROMPT_COUNT, BEAMS).astype(jnp.int32)


def level_of(own_key, shape, cuts, low, largest):
    level = 1.0
    for axis_at, parts in cuts:
        steps = jax.random.uniform(jax.random.fold_in(jax.random.fold_in(own_key, 6), axis_at), (parts,), jnp.float32, low / len(cuts), largest / len(cuts))
        level = level * jnp.repeat(jnp.exp(steps), shape[axis_at] // parts).reshape((-1,) + (1,) * (len(shape) - 1 - axis_at))
    return level


def centred(own_key, shape, spread, limit, shards=(), kind=jnp.bfloat16):
    values = jax.random.normal(own_key, shape, jnp.float32) * spread
    if len(shards) > 0:
        values = level_of(own_key, shape, shards, -0.22, 0.18) * values
    return jnp.clip(values, min=-limit, max=limit).astype(kind)


def setup_inputs(seed: int = 0) -> dict:
    streams_of = jax.random.split(jax.random.key(seed), 13)
    return {
        "prompt_queries": centred(streams_of[0], (PROMPT_COUNT, PROMPT_LENGTH, ATT), 1.0, 6.0, ((0, 16), (2, 2))),
        "prompt_keys": centred(streams_of[1], (PROMPT_COUNT, PROMPT_LENGTH, ATT), 1.0, 6.0, ((0, 16), (2, 2))),
        "prompt_values": centred(streams_of[2], (PROMPT_COUNT, PROMPT_LENGTH, ATT), 1.0, 6.0, ((0, 16), (2, 2))),
        "prompt_decay": draw_prompt_decay(jax.random.fold_in(streams_of[12], 71), 0),
        "prompt_lengths": draw_prompt_lengths(jax.random.fold_in(streams_of[12], 71), 0),
        "norm_gain": jnp.clip(1.0 + 0.18 * jax.random.normal(streams_of[5], (ATT,), jnp.float32), 0.1, 1.9),
        "decode_owner": draw_decode_owner(jax.random.fold_in(streams_of[12], 71), 0),
        "parent_beam": draw_parent_beam(jax.random.fold_in(streams_of[12], 71), 0),
        "step_queries": centred(streams_of[8], (DSTEPS, PROMPT_COUNT, BEAMS, ATT), 1.0, 6.0, ((1, 4), (2, 4), (3, 2))),
        "step_keys": centred(streams_of[9], (DSTEPS, PROMPT_COUNT, BEAMS, ATT), 2.0, 12.0, ((1, 4), (2, 4), (3, 2))),
        "step_values": centred(streams_of[10], (DSTEPS, PROMPT_COUNT, BEAMS, ATT), 2.0, 12.0, ((1, 4), (2, 4), (3, 2))),
        "step_decay": jnp.clip(-1.0 + 0.95 * jax.random.uniform(streams_of[11], (DSTEPS, PROMPT_COUNT, BEAMS, HEAD_COUNT), jnp.float32) ** level_of(streams_of[11], (DSTEPS, PROMPT_COUNT, BEAMS, HEAD_COUNT), ((1, 4), (3, 2)), -0.2, 0.2), -1.0, -0.05),
    }


highest = lax.Precision.HIGHEST
epsilon = 1e-06

def prefill_sequence(inputs, norm_gain):
    query_rows, key_rows, value_rows, decay_rows, length = inputs
    token_count = query_rows.shape[0]
    position_ids = jnp.arange(token_count, dtype=jnp.int32)
    live_mask = position_ids < length
    masked_decay = jnp.where(live_mask[None, :], decay_rows, jnp.float32(0.0))
    cumulative = jnp.cumsum(masked_decay, axis=1)
    queries = query_rows.reshape(token_count, HEAD_COUNT, HD).astype(jnp.float32)
    keys_live = jnp.where(live_mask[:, None], key_rows, jnp.zeros_like(key_rows)).reshape(token_count, HEAD_COUNT, HD).astype(jnp.float32)
    values = value_rows.reshape(token_count, HEAD_COUNT, HD).astype(jnp.float32)
    weights_end = jnp.exp(cumulative[:, -1:] - cumulative)
    final_state = jnp.einsum('thd,the->hde', keys_live * weights_end.T[:, :, None], values, precision=highest)
    carried_state = jnp.zeros((HEAD_COUNT, HD, HD), jnp.float32)
    inner_index = jnp.arange(BLK)
    causal = inner_index[:, None] >= inner_index[None, :]
    pieces = []
    block_total = token_count // BLK
    for block_index in range(block_total):
        block_start = block_index * BLK
        block_stop = block_start + BLK
        query_block = queries[block_start:block_stop]
        key_block = keys_live[block_start:block_stop]
        value_block = values[block_start:block_stop]
        block_cum = cumulative[:, block_start:block_stop]
        if block_index == 0:
            anchor = jnp.zeros((HEAD_COUNT,), jnp.float32)
        else:
            anchor = cumulative[:, block_start - 1]
        scores = jnp.einsum('thd,uhd->htu', query_block, key_block)
        exponent = jnp.where(causal[None], block_cum[:, :, None] - block_cum[:, None, :], -jnp.inf)
        weights = (scores * jnp.exp(exponent)).astype(jnp.bfloat16)
        local_part = jnp.einsum('htu,uhe->the', weights.astype(jnp.float32), value_block)
        lift_factor = jnp.exp(block_cum - anchor[:, None]).T[:, :, None]
        carried = jnp.einsum('thd,hde->the', query_block * lift_factor, carried_state, precision=highest)
        pieces.append(local_part + carried)
        if block_index + 1 < block_total:
            block_end = block_cum[:, -1]
            fade_factor = jnp.exp(block_end[:, None] - block_cum).T[:, :, None]
            carried_state = jnp.exp(block_end - anchor)[:, None, None] * carried_state + jnp.einsum('thd,the->hde', key_block * fade_factor, value_block, precision=highest)
    mixed = jnp.concatenate(pieces, axis=0).reshape(token_count, HEAD_COUNT * HD)
    mixed = jnp.where(live_mask[:, None], mixed, jnp.float32(0.0))
    mean_square = lax.optimization_barrier(jnp.mean(mixed * mixed, axis=-1))
    prompt_out = (mixed * lax.rsqrt(mean_square + epsilon)[:, None] * norm_gain).astype(jnp.bfloat16)
    return (prompt_out, final_state)

def outer_terms(key_rows, value_rows):
    return key_rows.astype(jnp.float32)[..., :, None] * value_rows.astype(jnp.float32)[..., None, :]

def decode_slot(inputs, prompt_state, norm_gain):
    sequence, parents, queries, keys_new, values_new, decays = inputs
    base_state = jnp.take(prompt_state, sequence, axis=0)
    shaped = (2, BEAMS, HEAD_COUNT, HD)
    queries = queries.reshape(shaped).astype(jnp.float32)
    keys_new = keys_new.reshape(shaped)
    values_new = values_new.reshape(shaped)
    first_state = jnp.exp(decays[0])[:, :, None, None] * base_state[None] + outer_terms(keys_new[0], values_new[0])
    first_mix = jnp.einsum('bhd,bhde->bhe', queries[0], first_state, precision=highest)
    parent_state = jnp.take(first_state, parents, axis=0)
    second_state = jnp.exp(decays[1])[:, :, None, None] * parent_state + outer_terms(keys_new[1], values_new[1])
    second_mix = jnp.einsum('bhd,bhde->bhe', queries[1], second_state, precision=highest)
    both_mix = jnp.stack([first_mix, second_mix]).reshape(2, BEAMS, HEAD_COUNT * HD)
    mean_square = lax.optimization_barrier(jnp.mean(both_mix * both_mix, axis=-1))
    return (both_mix * lax.rsqrt(mean_square + epsilon)[..., None] * norm_gain).astype(jnp.bfloat16)

def reference(prompt_queries, prompt_keys, prompt_values, prompt_decay, prompt_lengths, norm_gain, decode_owner, parent_beam, step_queries, step_keys, step_values, step_decay):
    prompt_out, prompt_state = lax.map(lambda inputs: prefill_sequence(inputs, norm_gain), (prompt_queries, prompt_keys, prompt_values, prompt_decay, prompt_lengths))
    seq_ids = jnp.arange(PROMPT_COUNT, dtype=jnp.int32)
    slot_order = jnp.argsort(decode_owner * PROMPT_COUNT + seq_ids).astype(jnp.int32)
    step_out = lax.map(lambda inputs: decode_slot(inputs, prompt_state, norm_gain), (slot_order, parent_beam, jnp.swapaxes(step_queries, 0, 1), jnp.swapaxes(step_keys, 0, 1), jnp.swapaxes(step_values, 0, 1), jnp.swapaxes(step_decay, 0, 1)))
    return (prompt_out, jnp.swapaxes(step_out, 0, 1))
```

```python
import functools
import math

import jax
import jax.numpy as jnp
from jax import lax
from jax.experimental import pallas as pl
from jax.experimental.pallas import tpu as pltpu
from jax.sharding import PartitionSpec as P

HEAD_COUNT = 64
HD = 128
BLK = 256
SUB = 128
LANES = 128
LOG2E = math.log2(math.e)
VMEM_BYTES = 56 * 1024 * 1024

highest = lax.Precision.HIGHEST
epsilon = 1e-06
f32 = jnp.float32
bf16 = jnp.bfloat16


def dot_nt(left, right, **more):
    return lax.dot_general(
        left, right, (((1,), (1,)), ((), ())), preferred_element_type=f32, **more
    )


def dot_tn(left, right):
    return lax.dot_general(left, right, (((0,), (0,)), ((), ())), preferred_element_type=f32)


def iota(shape, dim):
    return lax.broadcasted_iota(jnp.int32, shape, dim)


def states_kernel(heads, length_ref, decay_ref, keys_ref, values_ref, state_ref, final_ref, col_ref, row_ref):
    block = pl.program_id(0)
    live_row = block * BLK + iota((heads, BLK), 1) < length_ref[0]
    decay = jnp.where(live_row, decay_ref[...] * LOG2E, 0.0)
    later = iota((BLK, BLK), 0) <= iota((BLK, BLK), 1)
    row_ref[...] = jnp.dot(
        decay, later.astype(f32), precision=highest, preferred_element_type=f32
    )
    padded = jnp.concatenate([decay, jnp.zeros((LANES - heads, BLK), f32)], axis=0)
    earlier = iota((BLK, BLK), 1) <= iota((BLK, BLK), 0)
    col = dot_nt(earlier.astype(f32), padded, precision=highest)
    col_ref[...] = col
    end = col[BLK - 1 : BLK, :]
    live_col = block * BLK + iota((BLK, LANES), 0) < length_ref[0]
    fade = jnp.where(live_col, jnp.exp2(end - col), 0.0)
    keep = jnp.where(block == 0, 0.0, jnp.exp2(end))

    @pl.when(block == 0)
    def _():
        final_ref[...] = jnp.zeros_like(final_ref)

    for head in range(heads):
        span = slice(head * HD, (head + 1) * HD)
        faded = (keys_ref[:, span].astype(f32) * fade[:, head : head + 1]).astype(bf16)
        state = final_ref[head] * keep[:, head : head + 1] + dot_tn(values_ref[:, span], faded)
        final_ref[head] = state
        state_ref[0, head] = state.astype(bf16)


def prompt_states(lengths, decay, keys, values):
    heads, tokens = decay.shape
    columns = heads * HD
    blocks = tokens // BLK
    return pl.pallas_call(
        functools.partial(states_kernel, heads),
        grid=(blocks,),
        in_specs=[
            pl.BlockSpec(memory_space=pltpu.SMEM),
            pl.BlockSpec((heads, BLK), lambda b: (0, b)),
            pl.BlockSpec((BLK, columns), lambda b: (b, 0)),
            pl.BlockSpec((BLK, columns), lambda b: (b, 0)),
        ],
        out_specs=[
            pl.BlockSpec((1, heads, HD, HD), lambda b: (b, 0, 0, 0)),
            pl.BlockSpec((heads, HD, HD), lambda b: (0, 0, 0)),
            pl.BlockSpec((BLK, LANES), lambda b: (b, 0)),
            pl.BlockSpec((heads, BLK), lambda b: (0, b)),
        ],
        out_shape=[
            jax.ShapeDtypeStruct((blocks, heads, HD, HD), bf16),
            jax.ShapeDtypeStruct((heads, HD, HD), f32),
            jax.ShapeDtypeStruct((tokens, LANES), f32),
            jax.ShapeDtypeStruct((heads, tokens), f32),
        ],
        compiler_params=pltpu.CompilerParams(vmem_limit_bytes=VMEM_BYTES),
        cost_estimate=pl.CostEstimate(
            flops=2 * tokens * columns * HD,
            bytes_accessed=4 * tokens * columns + 2 * blocks * heads * HD * HD,
            transcendentals=0,
        ),
        name="prompt_states",
    )(lengths, decay, keys, values)


def mix_kernel(group, queries_ref, keys_ref, values_ref, state_ref, col_ref, row_ref, mixed_ref, sums_ref, total):
    block, part = pl.program_id(0), pl.program_id(1)
    shift = lax.rem(LANES - part * group, LANES)
    col_all = pltpu.roll(col_ref[...], shift, 1)
    lift_all = jnp.where(block == 0, 0.0, jnp.exp2(col_all))
    closed = jnp.where(iota((SUB, SUB), 1) <= iota((SUB, SUB), 0), 0.0, -jnp.inf)
    totals = [jnp.zeros((SUB, HD), f32), jnp.zeros((SUB, HD), f32)]
    for head in range(group):
        span = slice(head * HD, (head + 1) * HD)
        queries = queries_ref[:, span]
        keys = keys_ref[:, span]
        values = values_ref[:, span]
        state = state_ref[0, head]
        row = row_ref[head : head + 1, :]
        col = col_all[:, head : head + 1]
        lift = lift_all[:, head : head + 1]
        first = dot_nt(queries[:SUB], jnp.concatenate([keys[:SUB], state], axis=0))
        weights = first[:, :SUB] * jnp.exp2((col[:SUB] - row[:, :SUB]) + closed)
        mixed = jnp.dot(
            weights.astype(bf16), values[:SUB], preferred_element_type=f32
        ) + first[:, SUB:] * lift[:SUB]
        mixed_ref[:SUB, span] = mixed.astype(bf16)
        totals[0] = totals[0] + mixed * mixed
        second = dot_nt(queries[SUB:], keys)
        carried = dot_nt(queries[SUB:], state)
        gap = col[SUB:] - row
        gap = jnp.concatenate([gap[:, :SUB], gap[:, SUB:] + closed], axis=1)
        weights = second * jnp.exp2(gap)
        mixed = jnp.dot(
            weights.astype(bf16), values, preferred_element_type=f32
        ) + carried * lift[SUB:]
        mixed_ref[SUB:, span] = mixed.astype(bf16)
        totals[1] = totals[1] + mixed * mixed
    both = jnp.concatenate(totals, axis=0)

    @pl.when(part == 0)
    def _():
        total[...] = both

    @pl.when(part > 0)
    def _():
        total[...] += both

    @pl.when(part == pl.num_programs(1) - 1)
    def _():
        sums_ref[...] = dot_nt(jnp.ones((8, HD), f32), total[...], precision=highest)


def prompt_mix(queries, keys, values, state, col, row):
    tokens, columns = queries.shape
    heads = columns // HD
    group = min(8, heads)
    blocks = tokens // BLK
    wide = pl.BlockSpec((BLK, group * HD), lambda b, g: (b, g))
    return pl.pallas_call(
        functools.partial(mix_kernel, group),
        grid=(blocks, heads // group),
        in_specs=[
            wide,
            wide,
            wide,
            pl.BlockSpec((1, group, HD, HD), lambda b, g: (jnp.maximum(b - 1, 0), g, 0, 0)),
            pl.BlockSpec((BLK, LANES), lambda b, g: (b, 0)),
            pl.BlockSpec((group, BLK), lambda b, g: (g, b)),
        ],
        out_specs=[wide, pl.BlockSpec((8, BLK), lambda b, g: (0, b))],
        out_shape=[
            jax.ShapeDtypeStruct((tokens, columns), bf16),
            jax.ShapeDtypeStruct((8, tokens), f32),
        ],
        scratch_shapes=[pltpu.VMEM((BLK, HD), f32)],
        compiler_params=pltpu.CompilerParams(vmem_limit_bytes=VMEM_BYTES),
        cost_estimate=pl.CostEstimate(
            flops=2 * tokens * columns * 4 * HD,
            bytes_accessed=8 * tokens * columns,
            transcendentals=tokens * heads * BLK,
        ),
        name="prompt_mix",
    )(queries, keys, values, state, col, row)


def norm_kernel(width, count, length_ref, gain_ref, mixed_ref, *refs):
    block = pl.program_id(0)
    out_ref = refs[count]
    total = refs[0][...]
    for ref in refs[1:count]:
        total = total + ref[...]
    scale = lax.rsqrt(total * (1.0 / width) + epsilon)
    rows = scale.shape[1]
    scale = jnp.where(block * rows + iota(scale.shape, 1) < length_ref[0], scale, 0.0)
    scale = jnp.transpose(scale)[:, :1]
    out_ref[...] = (mixed_ref[...].astype(f32) * scale * gain_ref[...]).astype(bf16)


def prompt_norm(lengths, gain, mixed, sums):
    tokens, columns = mixed.shape
    wide = pl.BlockSpec((BLK, columns), lambda b: (b, 0))
    return pl.pallas_call(
        functools.partial(norm_kernel, HEAD_COUNT * HD, len(sums)),
        grid=(tokens // BLK,),
        in_specs=[
            pl.BlockSpec(memory_space=pltpu.SMEM),
            pl.BlockSpec((1, columns), lambda b: (0, 0)),
            wide,
        ]
        + [pl.BlockSpec((8, BLK), lambda b: (0, b))] * len(sums),
        out_specs=wide,
        out_shape=jax.ShapeDtypeStruct((tokens, columns), bf16),
        compiler_params=pltpu.CompilerParams(vmem_limit_bytes=VMEM_BYTES),
        cost_estimate=pl.CostEstimate(
            flops=3 * tokens * columns, bytes_accessed=4 * tokens * columns, transcendentals=0
        ),
        name="prompt_norm",
    )(lengths, gain, mixed, *sums)


def read_kernel(heads, count, *refs):
    state_ref = refs[count]
    outs = refs[count + 1 :]
    rows = refs[0].shape[0]
    for head in range(heads):
        span = slice(head * HD, (head + 1) * HD)
        state = state_ref[head]
        high = state.astype(bf16)
        low = (state - high.astype(f32)).astype(bf16)
        queries = jnp.concatenate([ref[:, span].astype(f32) for ref in refs[:count]], axis=0)
        queries = queries.astype(bf16)
        read = dot_nt(queries, high) + dot_nt(queries, low)
        for index, out in enumerate(outs):
            out[:, span] = read[index * rows : (index + 1) * rows].astype(bf16)


def read_states(queries, final_state):
    heads = final_state.shape[0]
    count = len(queries)
    return pl.pallas_call(
        functools.partial(read_kernel, heads, count),
        out_shape=[jax.ShapeDtypeStruct(queries[0].shape, bf16)] * count,
        compiler_params=pltpu.CompilerParams(vmem_limit_bytes=VMEM_BYTES),
        cost_estimate=pl.CostEstimate(
            flops=4 * count * queries[0].size * HD,
            bytes_accessed=4 * final_state.size + 4 * count * queries[0].size,
            transcendentals=0,
        ),
        name="read_states",
    )(*queries, final_state)


def steps_kernel(heads, queries_ref, keys_ref, values_ref, reads_ref, parent_keys_ref, parent_values_ref, first_ref, second_ref, mixed_ref, sums_ref):
    rows = queries_ref.shape[0]
    total = jnp.zeros((rows, HD), f32)
    for head in range(heads):
        span = slice(head * HD, (head + 1) * HD)
        queries = queries_ref[:, span].astype(f32)
        own = jnp.sum(queries * keys_ref[:, span].astype(f32), axis=1, keepdims=True)
        parent = jnp.sum(queries * parent_keys_ref[:, span].astype(f32), axis=1, keepdims=True)
        mixed = (
            first_ref[:, head : head + 1] * reads_ref[:, span].astype(f32)
            + own * values_ref[:, span].astype(f32)
            + second_ref[:, head : head + 1] * parent * parent_values_ref[:, span].astype(f32)
        )
        mixed_ref[:, span] = mixed
        total = total + mixed * mixed
    sums_ref[...] = jnp.broadcast_to(jnp.sum(total, axis=1, keepdims=True), sums_ref.shape)


def steps_mix(queries, keys, values, reads, parent_keys, parent_values, first, second):
    rows, columns = queries.shape
    return pl.pallas_call(
        functools.partial(steps_kernel, columns // HD),
        out_shape=[
            jax.ShapeDtypeStruct((rows, columns), f32),
            jax.ShapeDtypeStruct((rows, LANES), f32),
        ],
        compiler_params=pltpu.CompilerParams(vmem_limit_bytes=VMEM_BYTES),
        name="steps_mix",
    )(queries, keys, values, reads, parent_keys, parent_values, first, second)


def swap(array, axis, bit):
    size = lax.axis_size(axis)
    return lax.ppermute(array, axis, [(index, index ^ bit) for index in range(size)])


def over_pre(array):
    size = lax.axis_size("pre")
    return [array] + [swap(array, "pre", bit) for bit in range(1, size)]


def earlier_count(labels):
    total = labels.shape[-1]
    indices = jnp.arange(total, dtype=jnp.int32)
    before = indices[None, :] < indices[:, None]
    same_label = labels[..., :, None] == labels[..., None, :]
    return jnp.sum(jnp.where(same_label & before, 1, 0), axis=-1).astype(jnp.int32)


def pick_rows(matches, sources):
    return jnp.sum(jnp.where(matches, sources, 0), axis=-1)


def local(
    prompt_queries,
    prompt_keys,
    prompt_values,
    prompt_decay,
    prompt_lengths,
    norm_gain,
    decode_owner,
    parent_beam,
    step_queries,
    step_keys,
    step_values,
    step_decay,
):
    tokens, columns = prompt_queries.shape[1:]
    heads = prompt_decay.shape[1]
    steps, slots, per_block = step_queries.shape[:3]
    rows = steps * per_block
    group, block = lax.axis_index("grp"), lax.axis_index("dec")
    group_count, block_count = lax.axis_size("grp"), lax.axis_size("dec")
    seq_total = decode_owner.shape[0]
    near = group_count // 2

    def slot_major(array):
        return jnp.swapaxes(array, 0, 1).reshape(slots, rows, columns)

    queries = slot_major(step_queries)
    keys = slot_major(step_keys)
    values = slot_major(step_values)

    rank = earlier_count(decode_owner)
    slot_ids = jnp.arange(seq_total, dtype=jnp.int32)
    slot_of = decode_owner * slots + rank
    slot_order = pick_rows(slot_of[None, :] == slot_ids[:, None], slot_ids[None, :])
    around = block ^ jnp.arange(block_count, dtype=jnp.int32)

    def widen(array):
        pool = array
        bit = 1
        while bit < near:
            pool = jnp.concatenate([pool, swap(pool, "grp", bit)], axis=0)
            bit *= 2
        return pool

    def place(owner, index, count):
        offset = owner ^ group
        return jnp.where(offset < near, offset * count + index, 0), offset < near

    pool = widen(queries)
    theirs = (group ^ near) * block_count + around
    mine = group * block_count + around
    sent = jnp.take(pool, place(decode_owner[theirs], rank[theirs], slots)[0], axis=0)
    came = swap(sent, "grp", near)
    spot, here = place(decode_owner[mine], rank[mine], slots)
    for_prompts = jnp.where(here[:, None, None], jnp.take(pool, spot, axis=0), came)

    parent_rows = (
        parent_beam.reshape(slots, block_count, per_block)
        .transpose(1, 0, 2)
        .reshape(block_count, slots * per_block)
    )
    source_block = parent_rows // per_block
    slot_row = jnp.arange(slots * per_block, dtype=jnp.int32) // per_block * rows
    source_row = slot_row[None, :] + parent_rows % per_block
    row_rank = earlier_count(source_block)
    capacity = (slots + block_count - 2) // (block_count - 1)
    needed = source_block == block
    matches = needed[:, None, :] & (
        row_rank[:, None, :] == jnp.arange(capacity, dtype=jnp.int32)[None, :, None]
    )
    chosen = pick_rows(matches, source_row[:, None, :])[around]
    flat_keys = keys.reshape(slots * rows, columns)
    flat_values = values.reshape(slots * rows, columns)
    parcel_keys = jnp.take(flat_keys, chosen, axis=0)
    parcel_values = jnp.take(flat_values, chosen, axis=0)
    parcels = jnp.concatenate([parcel_keys, parcel_values], axis=1)

    query_parts, key_parts, value_parts = [for_prompts[0]], [], []
    split = columns * 2 * capacity // rows
    for bit in range(1, block_count):
        message = jnp.concatenate(
            [for_prompts[bit], parcels[bit].reshape(rows, split)], axis=1
        )
        message = swap(message, "dec", bit)
        query_parts.append(message[:, :columns])
        parcel = message[:, columns:].reshape(2 * capacity, columns)
        key_parts.append(parcel[:capacity])
        value_parts.append(parcel[capacity:])

    own_source = lax.dynamic_index_in_dim(source_block, block, 0, keepdims=False)
    own_rank = lax.dynamic_index_in_dim(row_rank, block, 0, keepdims=False)
    own_row = lax.dynamic_index_in_dim(source_row, block, 0, keepdims=False)
    away = (own_source ^ block) - 1
    parent_index = jnp.where(
        own_source == block, own_row, slots * rows + away * capacity + own_rank
    )
    parent_keys = jnp.take(jnp.concatenate([flat_keys] + key_parts), parent_index, axis=0)
    parent_values = jnp.take(jnp.concatenate([flat_values] + value_parts), parent_index, axis=0)

    def second_rows(array):
        array = array.reshape(slots, per_block, array.shape[-1])
        return jnp.pad(array, ((0, 0), (per_block, 0), (0, 0))).reshape(slots * rows, -1)

    parent_keys = second_rows(parent_keys)
    parent_values = second_rows(parent_values)

    own_decay = lax.dynamic_slice_in_dim(step_decay, block * per_block, per_block, 2)
    own_parents = lax.dynamic_slice_in_dim(parent_beam, block * per_block, per_block, 1)
    parent_decay = jnp.take_along_axis(step_decay[0], own_parents[:, :, None], axis=1)
    first = jnp.exp(jnp.stack([own_decay[0], own_decay[1] + parent_decay], axis=1))
    first = first.reshape(slots * rows, heads)
    second = second_rows(jnp.exp(own_decay[1]).reshape(slots * per_block, heads))

    state, final_state, col, row = prompt_states(
        prompt_lengths, prompt_decay[0], prompt_keys[0], prompt_values[0]
    )
    reads = read_states(query_parts, final_state)
    reads = [reads[0]] + [swap(reads[bit], "dec", bit) for bit in range(1, block_count)]
    pool = widen(jnp.stack(reads))

    def located(owner):
        prompts = lax.dynamic_slice_in_dim(slot_order, owner * slots, slots, 0)
        return place(prompts // block_count, (prompts % block_count) ^ block, block_count)

    sent = jnp.take(pool, located(group ^ near)[0], axis=0)
    came = swap(sent, "grp", near)
    spot, here = located(group)
    slot_reads = jnp.where(here[:, None, None], jnp.take(pool, spot, axis=0), came)

    mixed, sums = prompt_mix(
        prompt_queries[0], prompt_keys[0], prompt_values[0], state, col, row
    )
    prompt_out = prompt_norm(prompt_lengths, norm_gain[None], mixed, over_pre(sums))

    step_mixed, step_sums = steps_mix(
        queries.reshape(slots * rows, columns),
        flat_keys,
        flat_values,
        slot_reads.reshape(slots * rows, columns),
        parent_keys,
        parent_values,
        first,
        second,
    )
    step_total = functools.reduce(jnp.add, over_pre(step_sums[:, :1]))
    scale = lax.rsqrt(step_total / (HEAD_COUNT * HD) + epsilon)
    step_out = (step_mixed * scale * norm_gain).astype(bf16)
    step_out = jnp.swapaxes(step_out.reshape(slots, steps, per_block, columns), 0, 1)
    return (prompt_out[None], step_out)


def solution(mesh):
    in_specs = (
        P(("grp", "dec"), None, "pre"),
        P(("grp", "dec"), None, "pre"),
        P(("grp", "dec"), None, "pre"),
        P(("grp", "dec"), "pre", None),
        P(("grp", "dec")),
        P("pre"),
        P(),
        P("grp", None),
        P(None, "grp", "dec", "pre"),
        P(None, "grp", "dec", "pre"),
        P(None, "grp", "dec", "pre"),
        P(None, "grp", None, "pre"),
    )
    out_specs = (P(("grp", "dec"), None, "pre"), P(None, "grp", "dec", "pre"))
    return jax.shard_map(local, mesh=mesh, in_specs=in_specs, out_specs=out_specs, check_vma=False)
```

```python
import functools
import math

import jax
import jax.numpy as jnp
from jax import lax
from jax.experimental import pallas as pl
from jax.experimental.pallas import tpu as pltpu
from jax.sharding import PartitionSpec as P

HEAD_COUNT = 64
HD = 128
SUB = 128
LANES = 128
LOG2E = math.log2(math.e)
MIB = 1024 * 1024

highest = lax.Precision.HIGHEST
epsilon = 1e-06
f32 = jnp.float32
bf16 = jnp.bfloat16


def dot_nt(left, right, **more):
    return lax.dot_general(
        left, right, (((1,), (1,)), ((), ())), preferred_element_type=f32, **more
    )


def dot_tn(left, right):
    return lax.dot_general(left, right, (((0,), (0,)), ((), ())), preferred_element_type=f32)


def iota(shape, dim):
    return lax.broadcasted_iota(jnp.int32, shape, dim)


def pieces(array, count):
    parts = []
    for _ in range(count):
        part = array.astype(bf16)
        parts.append(part)
        array = array - part.astype(f32)
    return parts


def dot(left, right):
    return jnp.dot(left, right, preferred_element_type=f32)


def pass_kernel(heads, subs, each, length_ref, decay_ref, queries_ref, keys_ref, values_ref, after_ref, mixed_ref, sums_ref, state_ref, fade, lift, keep, total):
    step = pl.program_id(0)
    lower = iota((SUB, SUB), 1) <= iota((SUB, SUB), 0)

    @pl.when(step == 0)
    def _():
        upper = iota((SUB, SUB), 0) <= iota((SUB, SUB), 1)
        upper = upper.astype(f32).astype(bf16)
        earlier = lower.astype(f32).astype(bf16)
        rates, live = [], []
        for sub in range(subs):
            span = slice(sub * SUB, (sub + 1) * SUB)
            alive = sub * SUB + iota((heads, SUB), 1) < length_ref[0]
            rates.append(jnp.where(alive, decay_ref[:, span] * LOG2E, 0.0))
            live.append(alive)
        rates = jnp.concatenate(pieces(jnp.concatenate(rates, axis=0), 3), axis=1)
        row = dot(rates, jnp.concatenate([upper] * 3, axis=0))
        col = dot_nt(jnp.concatenate([earlier] * 3, axis=1), rates)
        half = 0.5 * row[:, SUB - 1 : SUB]
        fall = jnp.exp2(half - row)
        rise = jnp.exp2(col - 0.5 * col[SUB - 1 : SUB, :])
        scale = jnp.exp2(half)
        for sub in range(subs):
            span = slice(sub * heads, (sub + 1) * heads)
            fade[sub] = jnp.where(live[sub], fall[span], 0.0)
            lift[sub, :, :heads] = rise[:, span]
            after = scale[(sub + 1) * heads : (sub + 2) * heads] if sub + 1 < subs else 1.0
            keep[sub] = jnp.broadcast_to(scale[span] * after, (heads, LANES))
        state_ref[...] = jnp.zeros_like(state_ref)

    for index in range(each):
        sub = step * each + index
        rows = slice(index * SUB, (index + 1) * SUB)
        acc = jnp.zeros((SUB, HD), f32)
        for head in range(heads):
            span = slice(head * HD, (head + 1) * HD)
            queries = queries_ref[rows, span]
            values = values_ref[rows, span]
            keys = jnp.transpose(keys_ref[rows, span])
            weight = fade[sub, head : head + 1, :]
            faded = (keys.astype(f32) * weight).astype(bf16)
            scores = jnp.where(lower, dot(queries, keys) * weight, 0.0).astype(bf16)
            state = state_ref[head]
            mixed = dot(
                jnp.concatenate([scores, queries], axis=1),
                jnp.concatenate([values, state.astype(bf16)], axis=0),
            )
            mixed = mixed * lift[sub, :, head : head + 1]
            state_ref[head] = (state + dot(faded, values)) * keep[sub, head : head + 1, :]
            mixed_ref[rows, span] = mixed.astype(bf16)
            acc = acc + mixed * mixed
        total[pl.ds(pl.multiple_of(sub * SUB, SUB), SUB), :] = acc

    @pl.when(step == subs // each - 1)
    def _():
        sums_ref[...] = dot_nt(
            jnp.ones((8, 2 * HD), bf16), jnp.concatenate(pieces(total[...], 2), axis=1)
        )


def prompt_pass(lengths, decay, queries, keys, values, after):
    heads, tokens = decay.shape
    columns = heads * HD
    subs = tokens // SUB
    each = 2
    wide = pl.BlockSpec((SUB * each, columns), lambda b: (b, 0))
    return pl.pallas_call(
        functools.partial(pass_kernel, heads, subs, each),
        grid=(subs // each,),
        in_specs=[
            pl.BlockSpec(memory_space=pltpu.SMEM),
            pl.BlockSpec((heads, tokens), lambda b: (0, 0)),
            wide,
            wide,
            wide,
            pl.BlockSpec(memory_space=pl.ANY),
        ],
        out_specs=[
            wide,
            pl.BlockSpec((8, tokens), lambda b: (0, 0)),
            pl.BlockSpec((heads, HD, HD), lambda b: (0, 0, 0)),
        ],
        out_shape=[
            jax.ShapeDtypeStruct((tokens, columns), bf16),
            jax.ShapeDtypeStruct((8, tokens), f32),
            jax.ShapeDtypeStruct((heads, HD, HD), f32),
        ],
        scratch_shapes=[
            pltpu.VMEM((subs, heads, LANES), f32),
            pltpu.VMEM((subs, SUB, LANES), f32),
            pltpu.VMEM((subs, heads, LANES), f32),
            pltpu.VMEM((tokens, HD), f32),
        ],
        compiler_params=pltpu.CompilerParams(vmem_limit_bytes=48 * MIB),
        cost_estimate=pl.CostEstimate(
            flops=8 * tokens * columns * HD, bytes_accessed=8 * tokens * columns, transcendentals=0
        ),
        name="prompt_pass",
    )(lengths, decay, queries, keys, values, after)


def norm_kernel(width, count, base, length_ref, gain_ref, mixed_ref, *refs):
    block = pl.program_id(0)
    out_ref = refs[-1]
    total = refs[0][...]
    for ref in refs[1:count]:
        total = total + ref[...]
    scale = lax.rsqrt(total * (1.0 / width) + epsilon)
    rows = scale.shape[1]
    scale = jnp.where(base + block * rows + iota(scale.shape, 1) < length_ref[0], scale, 0.0)
    scale = jnp.transpose(scale)[:, :1]
    for column in range(0, gain_ref.shape[1], 512):
        span = slice(column, column + 512)
        out_ref[:, span] = (
            mixed_ref[:, span].astype(f32) * scale * gain_ref[:, span]
        ).astype(bf16)


def prompt_norm(lengths, gain, mixed, sums, base, rows, out, after):
    tokens, columns = mixed.shape
    skip = base // SUB
    spare = pl.BlockSpec(memory_space=pl.ANY)
    more = [after] if out is None else [after, out]
    return pl.pallas_call(
        functools.partial(norm_kernel, HEAD_COUNT * HD, len(sums), base),
        grid=(rows // SUB,),
        in_specs=[
            pl.BlockSpec(memory_space=pltpu.SMEM),
            pl.BlockSpec((1, columns), lambda b: (0, 0)),
            pl.BlockSpec((SUB, columns), lambda b: (b + skip, 0)),
        ]
        + [pl.BlockSpec((8, SUB), lambda b: (0, b + skip))] * len(sums)
        + [spare] * len(more),
        out_specs=pl.BlockSpec((SUB, columns), lambda b: (b + skip, 0)),
        out_shape=jax.ShapeDtypeStruct((tokens, columns), bf16),
        input_output_aliases={} if out is None else {4 + len(sums): 0},
        compiler_params=pltpu.CompilerParams(vmem_limit_bytes=12 * MIB),
        cost_estimate=pl.CostEstimate(
            flops=3 * rows * columns, bytes_accessed=4 * rows * columns, transcendentals=0
        ),
        name="prompt_norm",
    )(lengths, gain, mixed, *sums, *more)


def read_kernel(heads, count, *refs):
    state_ref = refs[count]
    outs = refs[count + 1 :]
    rows = refs[0].shape[0]
    for head in range(heads):
        span = slice(head * HD, (head + 1) * HD)
        high, low = pieces(state_ref[head], 2)
        queries = jnp.concatenate([ref[:, span].astype(f32) for ref in refs[:count]], axis=0)
        queries = queries.astype(bf16)
        read = dot(
            jnp.concatenate([queries, queries], axis=1), jnp.concatenate([high, low], axis=0)
        )
        for index, out in enumerate(outs):
            out[:, span] = read[index * rows : (index + 1) * rows].astype(bf16)


def read_states(queries, state):
    heads = state.shape[0]
    count = len(queries)
    rows = queries[0].shape[0]
    group = min(8, heads)
    part = pl.BlockSpec((rows, group * HD), lambda g: (0, g))
    return pl.pallas_call(
        functools.partial(read_kernel, group, count),
        grid=(heads // group,),
        in_specs=[part] * count + [pl.BlockSpec((group, HD, HD), lambda g: (g, 0, 0))],
        out_specs=[part] * count,
        out_shape=[jax.ShapeDtypeStruct((rows, heads * HD), bf16)] * count,
        compiler_params=pltpu.CompilerParams(vmem_limit_bytes=12 * MIB),
        cost_estimate=pl.CostEstimate(
            flops=4 * count * rows * heads * HD * HD,
            bytes_accessed=4 * state.size + 4 * count * rows * heads * HD,
            transcendentals=0,
        ),
        name="read_states",
    )(*queries, state)


def rank_of(owner_ref, prompt):
    owner = owner_ref[prompt]
    rank = jnp.int32(0)
    for other in range(owner_ref.shape[0]):
        rank = rank + jnp.where((owner_ref[other] == owner) & (other < prompt), 1, 0)
    return owner, rank


def prompts_of(owner_ref, owner, slots):
    found = [jnp.int32(0)] * slots
    seen = jnp.int32(0)
    for prompt in range(owner_ref.shape[0]):
        mine = owner_ref[prompt] == owner
        found = [
            jnp.where(mine & (seen == slot), prompt, one) for slot, one in enumerate(found)
        ]
        seen = seen + jnp.where(mine, 1, 0)
    return found


def copy_one(choice, pool, write):
    for index, take in enumerate(pool):

        @pl.when(choice == index)
        def _(take=take):
            write(take())


def ask_kernel(near, owner_ref, place_ref, *refs):
    pool, out_ref = refs[:near], refs[near]
    group, block = place_ref[0], place_ref[1]
    count = out_ref.shape[0]
    for bit in range(count):
        owner, rank = rank_of(owner_ref, (group ^ near) * count + (block ^ bit))
        offset = owner ^ group

        def write(value, bit=bit):
            out_ref[bit] = value

        copy_one(offset, [lambda ref=ref, rank=rank: ref[rank] for ref in pool], write)


def ask(owner, place, pool, count):
    whole = pl.BlockSpec(memory_space=pltpu.VMEM)
    scalar = pl.BlockSpec(memory_space=pltpu.SMEM)
    return pl.pallas_call(
        functools.partial(ask_kernel, len(pool)),
        in_specs=[scalar, scalar] + [whole] * len(pool),
        out_specs=whole,
        out_shape=jax.ShapeDtypeStruct((count,) + pool[0].shape[1:], bf16),
        compiler_params=pltpu.CompilerParams(vmem_limit_bytes=8 * MIB),
        name="ask",
    )(owner, place, *pool)


def one_hot(mask):
    return mask.astype(f32).astype(bf16)


def parcel_kernel(near, slots, capacity, owner_ref, place_ref, parent_ref, *refs):
    pool, (came_ref, keys_ref, values_ref) = refs[:near], refs[near : near + 3]
    outs = refs[near + 3 :]
    group, block = place_ref[0], place_ref[1]
    count = len(outs)
    rows, columns = outs[0].shape
    per_block = rows // 2
    halves = rows // (2 * capacity)
    split = columns // halves
    lines = slots * rows
    for bit, out in enumerate(outs):
        owner, rank = rank_of(owner_ref, group * count + (block ^ bit))
        choice = jnp.minimum(owner ^ group, near)

        def write(value, out=out):
            out[:, :columns] = value

        copy_one(
            choice,
            [lambda ref=ref, rank=rank: ref[rank] for ref in pool]
            + [lambda bit=bit: came_ref[bit]],
            write,
        )
        if bit == 0:
            continue
        target = block ^ bit
        seen = jnp.int32(0)
        sources = [jnp.int32(0)] * capacity
        for slot in range(slots):
            for beam in range(per_block):
                parent = parent_ref[slot, target * per_block + beam]
                hit = lax.div(parent, per_block) == block
                row = slot * rows + parent - block * per_block
                sources = [
                    jnp.where(hit & (seen == index), row, one)
                    for index, one in enumerate(sources)
                ]
                seen = seen + jnp.where(hit, 1, 0)
        line, source = iota((rows, lines), 0), iota((rows, lines), 1)
        parcel = jnp.zeros((rows, split), f32)
        for half in range(halves):
            span = slice(half * split, (half + 1) * split)
            first = half * 2 * capacity
            for kind, ref in enumerate((keys_ref, values_ref)):
                mask = (line == first + kind * capacity) & (source == sources[0])
                for index in range(1, capacity):
                    mask = mask | (
                        (line == first + kind * capacity + index) & (source == sources[index])
                    )
                parcel = parcel + dot(one_hot(mask), ref[:, span])
        out[:, columns:] = parcel.astype(bf16)


def parcels(owner, place, parents, pool, came, keys, values, capacity):
    whole = pl.BlockSpec(memory_space=pltpu.VMEM)
    scalar = pl.BlockSpec(memory_space=pltpu.SMEM)
    count, rows, columns = came.shape
    wide = columns + columns * 2 * capacity // rows
    return pl.pallas_call(
        functools.partial(parcel_kernel, len(pool), parents.shape[0], capacity),
        in_specs=[scalar] * 3 + [whole] * (len(pool) + 3),
        out_specs=[whole] * count,
        out_shape=[
            jax.ShapeDtypeStruct((rows, wide if bit else columns), bf16) for bit in range(count)
        ],
        compiler_params=pltpu.CompilerParams(vmem_limit_bytes=12 * MIB),
        name="parcels",
    )(owner, place, parents, *pool, came, keys, values)


def reply_kernel(near, owner_ref, place_ref, *refs):
    pool, out_ref = refs[:-1], refs[-1]
    group, block = place_ref[0], place_ref[1]
    count = len(pool) // near
    for slot, prompt in enumerate(prompts_of(owner_ref, group ^ near, out_ref.shape[0])):
        offset = lax.div(prompt, count) ^ group
        choice = offset * count + (lax.rem(prompt, count) ^ block)

        def write(value, slot=slot):
            out_ref[slot] = value

        copy_one(choice, [lambda ref=ref: ref[...] for ref in pool], write)


def reply(owner, place, pool, near, slots):
    whole = pl.BlockSpec(memory_space=pltpu.VMEM)
    scalar = pl.BlockSpec(memory_space=pltpu.SMEM)
    return pl.pallas_call(
        functools.partial(reply_kernel, near),
        in_specs=[scalar, scalar] + [whole] * len(pool),
        out_specs=whole,
        out_shape=jax.ShapeDtypeStruct((slots,) + pool[0].shape, bf16),
        compiler_params=pltpu.CompilerParams(vmem_limit_bytes=8 * MIB),
        name="reply",
    )(owner, place, *pool)


def terms_kernel(slots, capacity, count, place_ref, parent_ref, decay_ref, queries_ref, keys_ref, values_ref, *refs):
    far = refs[:count]
    terms_ref, first_ref, second, parent_keys, parent_values = refs[count + 1 :]
    block = place_ref[1]
    lines, columns = queries_ref.shape
    heads = columns // HD
    rows = lines // slots
    per_block = rows // 2
    halves = rows // (2 * capacity)
    split = columns // halves
    line = iota((lines, LANES), 0)
    near_col = jnp.full((lines, LANES), -1, jnp.int32)
    far_col = jnp.full((lines, LANES), -1, jnp.int32)
    sources = []
    for slot in range(slots):
        for beam in range(per_block):
            parent = parent_ref[slot, block * per_block + beam]
            source = lax.div(parent, per_block)
            rank = jnp.int32(0)
            for other in sources:
                rank = rank + jnp.where(other == source, 1, 0)
            sources.append(source)
            away = source ^ block
            near_at = slot * rows + parent - source * per_block
            near_at = jnp.where(away == 0, near_at, -1)
            far_at = jnp.where(away == 0, -1, (away - 1) * rows + rank)
            here = line == slot * rows + per_block + beam
            near_col = jnp.where(here, near_at, near_col)
            far_col = jnp.where(here, far_at, far_col)
            own = block * per_block + beam
            now = slot * rows + beam
            then = now + per_block
            step_one = decay_ref[1, slot, pl.ds(own, 1), :]
            first_ref[now : now + 1, :] = decay_ref[0, slot, pl.ds(own, 1), :]
            first_ref[then : then + 1, :] = step_one + decay_ref[0, slot, pl.ds(parent, 1), :]
            second[now : now + 1, :] = jnp.full_like(step_one, -1e30)
            second[then : then + 1, :] = step_one
    first_ref[...] = jnp.exp(first_ref[...])
    second[...] = jnp.exp(second[...])
    own_hot = one_hot(iota((lines, lines), 1) == near_col[:, :lines])
    column = iota((lines, rows), 1)
    for half in range(halves):
        span = slice(half * split, (half + 1) * split)
        for kind, (ref, store) in enumerate(
            ((keys_ref, parent_keys), (values_ref, parent_values))
        ):
            picked = dot(own_hot, ref[:, span])
            for index, message in enumerate(far):
                low, high = half * 2 * capacity, kind * capacity
                hot = (column == far_col[:, :rows] - index * rows + low + high) & (
                    (far_col[:, :rows] >= index * rows)
                    & (far_col[:, :rows] < index * rows + capacity)
                )
                picked = picked + dot(one_hot(hot), message[:, columns:])
            store[:, span] = picked
    for head in range(heads):
        span = slice(head * HD, (head + 1) * HD)
        queries = queries_ref[:, span].astype(f32)
        own = jnp.sum(queries * keys_ref[:, span].astype(f32), axis=1, keepdims=True)
        parent = jnp.sum(queries * parent_keys[:, span], axis=1, keepdims=True)
        terms_ref[:, span] = own * values_ref[:, span].astype(f32) + (
            second[:, head : head + 1] * parent
        ) * parent_values[:, span]


def step_terms(place, parents, decay, queries, keys, values, far, capacity, after):
    lines, columns = queries.shape
    heads = columns // HD
    whole = pl.BlockSpec(memory_space=pltpu.VMEM)
    scalar = pl.BlockSpec(memory_space=pltpu.SMEM)
    return pl.pallas_call(
        functools.partial(terms_kernel, parents.shape[0], capacity, len(far)),
        in_specs=[scalar] * 2
        + [whole] * (4 + len(far))
        + [pl.BlockSpec(memory_space=pl.ANY)],
        out_shape=[
            jax.ShapeDtypeStruct((lines, columns), f32),
            jax.ShapeDtypeStruct((lines, heads), f32),
        ],
        scratch_shapes=[
            pltpu.VMEM((lines, heads), f32),
            pltpu.VMEM((lines, columns), f32),
            pltpu.VMEM((lines, columns), f32),
        ],
        compiler_params=pltpu.CompilerParams(vmem_limit_bytes=12 * MIB),
        name="step_terms",
    )(place, parents, decay, queries, keys, values, *far, after)


def steps_kernel(heads, near, owner_ref, place_ref, *refs):
    pool = refs[:-5]
    came_ref, terms_ref, first_ref, mixed_ref, sums_ref = refs[-5:]
    group, block = place_ref[0], place_ref[1]
    count = len(pool) // near
    slots, rows = came_ref.shape[:2]
    for slot, prompt in enumerate(prompts_of(owner_ref, group, slots)):
        offset = lax.div(prompt, count) ^ group
        choice = offset * count + (lax.rem(prompt, count) ^ block)
        lines = slice(slot * rows, (slot + 1) * rows)
        total = jnp.zeros((rows, HD), f32)
        for head in range(heads):
            span = slice(head * HD, (head + 1) * HD)
            read = came_ref[slot, :, span].astype(f32)
            for index in range(len(pool)):
                read = jnp.where(choice == index, pool[index][:, span].astype(f32), read)
            mixed = first_ref[lines, head : head + 1] * read + terms_ref[lines, span]
            mixed_ref[lines, span] = mixed
            total = total + mixed * mixed
        sums_ref[lines, :] = jnp.broadcast_to(
            jnp.sum(total, axis=1, keepdims=True), (rows, LANES)
        )


def steps_mix(owner, place, pool, near, came, terms, first):
    lines, columns = terms.shape
    whole = pl.BlockSpec(memory_space=pltpu.VMEM)
    scalar = pl.BlockSpec(memory_space=pltpu.SMEM)
    return pl.pallas_call(
        functools.partial(steps_kernel, columns // HD, near),
        in_specs=[scalar, scalar] + [whole] * (len(pool) + 3),
        out_shape=[
            jax.ShapeDtypeStruct((lines, columns), f32),
            jax.ShapeDtypeStruct((lines, LANES), f32),
        ],
        compiler_params=pltpu.CompilerParams(vmem_limit_bytes=12 * MIB),
        name="steps_mix",
    )(owner, place, *pool, came, terms, first)


def swap(array, axis, bit):
    size = lax.axis_size(axis)
    return lax.ppermute(array, axis, [(index, index ^ bit) for index in range(size)])


def over_pre(array):
    size = lax.axis_size("pre")
    return [array] + [swap(array, "pre", bit) for bit in range(1, size)]


def local(
    prompt_queries,
    prompt_keys,
    prompt_values,
    prompt_decay,
    prompt_lengths,
    norm_gain,
    decode_owner,
    parent_beam,
    step_queries,
    step_keys,
    step_values,
    step_decay,
):
    tokens, columns = prompt_queries.shape[1:]
    heads = prompt_decay.shape[1]
    steps, slots, per_block = step_queries.shape[:3]
    rows = steps * per_block
    group, block = lax.axis_index("grp"), lax.axis_index("dec")
    group_count, block_count = lax.axis_size("grp"), lax.axis_size("dec")
    near = group_count // 2

    def slot_major(array):
        return jnp.swapaxes(array, 0, 1).reshape(slots, rows, columns)

    def widen(pool):
        bit = 1
        while bit < near:
            pool = pool + [swap(one, "grp", bit) for one in pool]
            bit *= 2
        return pool

    place = jnp.stack([group, block]).astype(jnp.int32)
    capacity = (slots + block_count - 2) // (block_count - 1)

    queries = slot_major(step_queries)
    asked = widen([queries])
    sent = ask(decode_owner, place, asked, block_count)
    came = swap(sent, "grp", near)
    mixed, sums, state = prompt_pass(
        prompt_lengths, prompt_decay[0], prompt_queries[0], prompt_keys[0], prompt_values[0], sent
    )
    came, step_keys, step_values, sums = lax.optimization_barrier(
        (came, step_keys, step_values, sums)
    )
    queries = queries.reshape(slots * rows, columns)
    keys = slot_major(step_keys).reshape(slots * rows, columns)
    values = slot_major(step_values).reshape(slots * rows, columns)

    messages = parcels(
        decode_owner, place, parent_beam, asked, came, keys, values, capacity
    )
    far = [swap(messages[bit], "dec", bit) for bit in range(1, block_count)]
    squares = over_pre(sums)
    share = tokens // 2
    prompt_out = prompt_norm(
        prompt_lengths, norm_gain[None], mixed, squares, 0, share, None, messages[-1]
    )
    state, prompt_out = lax.optimization_barrier((state, prompt_out))
    reads = read_states([messages[0]] + far, state)
    prompt_out = prompt_norm(
        prompt_lengths, norm_gain[None], mixed, squares, share, share, prompt_out, reads[-1]
    )
    reads = [reads[0]] + [swap(reads[bit], "dec", bit) for bit in range(1, block_count)]
    reads, prompt_out = lax.optimization_barrier((reads, prompt_out))
    pool = widen(reads)
    sent = reply(decode_owner, place, pool, near, slots)
    came = swap(sent, "grp", near)
    terms, first = step_terms(
        place, parent_beam, step_decay, queries, keys, values, far, capacity, sent
    )
    step_mixed, step_sums = steps_mix(decode_owner, place, pool, near, came, terms, first)
    step_total = functools.reduce(jnp.add, over_pre(step_sums[:, :1]))
    scale = lax.rsqrt(step_total / (HEAD_COUNT * HD) + epsilon)
    step_out = (step_mixed * scale * norm_gain).astype(bf16)
    step_out = jnp.swapaxes(step_out.reshape(slots, steps, per_block, columns), 0, 1)
    return (prompt_out[None], step_out)


def solution(mesh):
    in_specs = (
        P(("grp", "dec"), None, "pre"),
        P(("grp", "dec"), None, "pre"),
        P(("grp", "dec"), None, "pre"),
        P(("grp", "dec"), "pre", None),
        P(("grp", "dec")),
        P("pre"),
        P(),
        P("grp", None),
        P(None, "grp", "dec", "pre"),
        P(None, "grp", "dec", "pre"),
        P(None, "grp", "dec", "pre"),
        P(None, "grp", None, "pre"),
    )
    out_specs = (P(("grp", "dec"), None, "pre"), P(None, "grp", "dec", "pre"))
    return jax.shard_map(local, mesh=mesh, in_specs=in_specs, out_specs=out_specs, check_vma=False)
```

```python
import functools
import math

import jax
import jax.numpy as jnp
from jax import lax
from jax.experimental import pallas as pl
from jax.experimental.pallas import tpu as pltpu
from jax.sharding import PartitionSpec as P

HEAD_COUNT = 64
HD = 128
SUB = 128
LANES = 128
LOG2E = math.log2(math.e)
MIB = 1024 * 1024

highest = lax.Precision.HIGHEST
epsilon = 1e-06
f32 = jnp.float32
bf16 = jnp.bfloat16


def dot_nt(left, right, **more):
    return lax.dot_general(
        left, right, (((1,), (1,)), ((), ())), preferred_element_type=f32, **more
    )


def dot_tn(left, right):
    return lax.dot_general(left, right, (((0,), (0,)), ((), ())), preferred_element_type=f32)


def iota(shape, dim):
    return lax.broadcasted_iota(jnp.int32, shape, dim)


def pieces(array, count):
    parts = []
    for _ in range(count):
        part = array.astype(bf16)
        parts.append(part)
        array = array - part.astype(f32)
    return parts


def dot(left, right):
    return jnp.dot(left, right, preferred_element_type=f32)


def pass_kernel(heads, subs, each, length_ref, decay_ref, queries_ref, keys_ref, values_ref, after_ref, mixed_ref, sums_ref, state_ref, fade, lift, keep, total):
    step = pl.program_id(0)
    lower = iota((SUB, SUB), 1) <= iota((SUB, SUB), 0)

    @pl.when(step == 0)
    def _():
        upper = iota((SUB, SUB), 0) <= iota((SUB, SUB), 1)
        upper = upper.astype(f32).astype(bf16)
        earlier = lower.astype(f32).astype(bf16)
        rates, live = [], []
        for sub in range(subs):
            span = slice(sub * SUB, (sub + 1) * SUB)
            alive = sub * SUB + iota((heads, SUB), 1) < length_ref[0]
            rates.append(jnp.where(alive, decay_ref[:, span] * LOG2E, 0.0))
            live.append(alive)
        rates = jnp.concatenate(pieces(jnp.concatenate(rates, axis=0), 3), axis=1)
        row = dot(rates, jnp.concatenate([upper] * 3, axis=0))
        col = dot_nt(jnp.concatenate([earlier] * 3, axis=1), rates)
        half = 0.5 * row[:, SUB - 1 : SUB]
        fall = jnp.exp2(half - row)
        rise = jnp.exp2(col - 0.5 * col[SUB - 1 : SUB, :])
        scale = jnp.exp2(half)
        for sub in range(subs):
            span = slice(sub * heads, (sub + 1) * heads)
            fade[sub] = jnp.where(live[sub], fall[span], 0.0)
            lift[sub, :, :heads] = rise[:, span]
            after = scale[(sub + 1) * heads : (sub + 2) * heads] if sub + 1 < subs else 1.0
            keep[sub] = jnp.broadcast_to(scale[span] * after, (heads, LANES))
        state_ref[...] = jnp.zeros_like(state_ref)

    for index in range(each):
        sub = step * each + index
        rows = slice(index * SUB, (index + 1) * SUB)
        acc = jnp.zeros((SUB, HD), f32)
        for head in range(heads):
            span = slice(head * HD, (head + 1) * HD)
            queries = queries_ref[rows, span]
            values = values_ref[rows, span]
            keys = jnp.transpose(keys_ref[rows, span])
            weight = fade[sub, head : head + 1, :]
            faded = (keys.astype(f32) * weight).astype(bf16)
            scores = jnp.where(lower, dot(queries, keys) * weight, 0.0).astype(bf16)
            state = state_ref[head]
            mixed = dot(
                jnp.concatenate([scores, queries], axis=1),
                jnp.concatenate([values, state.astype(bf16)], axis=0),
            )
            mixed = mixed * lift[sub, :, head : head + 1]
            state_ref[head] = (state + dot(faded, values)) * keep[sub, head : head + 1, :]
            mixed_ref[rows, span] = mixed.astype(bf16)
            acc = acc + mixed * mixed
        total[pl.ds(pl.multiple_of(sub * SUB, SUB), SUB), :] = acc

    @pl.when(step == subs // each - 1)
    def _():
        sums_ref[...] = dot_nt(
            jnp.ones((8, 2 * HD), bf16), jnp.concatenate(pieces(total[...], 2), axis=1)
        )


def prompt_pass(lengths, decay, queries, keys, values, after):
    heads, tokens = decay.shape
    columns = heads * HD
    subs = tokens // SUB
    each = 2
    wide = pl.BlockSpec((SUB * each, columns), lambda b: (b, 0))
    return pl.pallas_call(
        functools.partial(pass_kernel, heads, subs, each),
        grid=(subs // each,),
        in_specs=[
            pl.BlockSpec(memory_space=pltpu.SMEM),
            pl.BlockSpec((heads, tokens), lambda b: (0, 0)),
            wide,
            wide,
            wide,
            pl.BlockSpec(memory_space=pl.ANY),
        ],
        out_specs=[
            wide,
            pl.BlockSpec((8, tokens), lambda b: (0, 0)),
            pl.BlockSpec((heads, HD, HD), lambda b: (0, 0, 0)),
        ],
        out_shape=[
            jax.ShapeDtypeStruct((tokens, columns), bf16),
            jax.ShapeDtypeStruct((8, tokens), f32),
            jax.ShapeDtypeStruct((heads, HD, HD), f32),
        ],
        scratch_shapes=[
            pltpu.VMEM((subs, heads, LANES), f32),
            pltpu.VMEM((subs, SUB, LANES), f32),
            pltpu.VMEM((subs, heads, LANES), f32),
            pltpu.VMEM((tokens, HD), f32),
        ],
        compiler_params=pltpu.CompilerParams(vmem_limit_bytes=48 * MIB),
        cost_estimate=pl.CostEstimate(
            flops=8 * tokens * columns * HD, bytes_accessed=8 * tokens * columns, transcendentals=0
        ),
        name="prompt_pass",
    )(lengths, decay, queries, keys, values, after)


def norm_kernel(width, count, base, length_ref, gain_ref, mixed_ref, *refs):
    block = pl.program_id(0)
    out_ref = refs[-1]
    total = refs[0][...]
    for ref in refs[1:count]:
        total = total + ref[...]
    scale = lax.rsqrt(total * (1.0 / width) + epsilon)
    rows = scale.shape[1]
    scale = jnp.where(base + block * rows + iota(scale.shape, 1) < length_ref[0], scale, 0.0)
    scale = jnp.transpose(scale)[:, :1]
    for column in range(0, gain_ref.shape[1], 512):
        span = slice(column, column + 512)
        out_ref[:, span] = (
            mixed_ref[:, span].astype(f32) * scale * gain_ref[:, span]
        ).astype(bf16)


def prompt_norm(lengths, gain, mixed, sums, base, rows, out, after, room=50):
    tokens, columns = mixed.shape
    skip = base // SUB
    spare = pl.BlockSpec(memory_space=pl.ANY)
    more = [after] if out is None else [after, out]
    return pl.pallas_call(
        functools.partial(norm_kernel, HEAD_COUNT * HD, len(sums), base),
        grid=(rows // SUB,),
        in_specs=[
            pl.BlockSpec(memory_space=pltpu.SMEM),
            pl.BlockSpec((1, columns), lambda b: (0, 0)),
            pl.BlockSpec((SUB, columns), lambda b: (b + skip, 0)),
        ]
        + [pl.BlockSpec((8, SUB), lambda b: (0, b + skip))] * len(sums)
        + [spare] * len(more),
        out_specs=pl.BlockSpec((SUB, columns), lambda b: (b + skip, 0)),
        out_shape=jax.ShapeDtypeStruct((tokens, columns), bf16),
        input_output_aliases={} if out is None else {4 + len(sums): 0},
        compiler_params=pltpu.CompilerParams(vmem_limit_bytes=room * MIB),
        cost_estimate=pl.CostEstimate(
            flops=3 * rows * columns, bytes_accessed=4 * rows * columns, transcendentals=0
        ),
        name="prompt_norm",
    )(lengths, gain, mixed, *sums, *more)


def read_kernel(heads, count, *refs):
    state_ref = refs[count]
    outs = refs[count + 1 :]
    rows = refs[0].shape[0]
    for head in range(heads):
        span = slice(head * HD, (head + 1) * HD)
        high, low = pieces(state_ref[head], 2)
        queries = jnp.concatenate([ref[:, span].astype(f32) for ref in refs[:count]], axis=0)
        queries = queries.astype(bf16)
        read = dot(
            jnp.concatenate([queries, queries], axis=1), jnp.concatenate([high, low], axis=0)
        )
        for index, out in enumerate(outs):
            out[:, span] = read[index * rows : (index + 1) * rows].astype(bf16)


def read_states(queries, state):
    heads = state.shape[0]
    count = len(queries)
    rows = queries[0].shape[0]
    group = min(8, heads)
    part = pl.BlockSpec((rows, group * HD), lambda g: (0, g))
    return pl.pallas_call(
        functools.partial(read_kernel, group, count),
        grid=(heads // group,),
        in_specs=[part] * count + [pl.BlockSpec((group, HD, HD), lambda g: (g, 0, 0))],
        out_specs=[part] * count,
        out_shape=[jax.ShapeDtypeStruct((rows, heads * HD), bf16)] * count,
        compiler_params=pltpu.CompilerParams(vmem_limit_bytes=12 * MIB),
        cost_estimate=pl.CostEstimate(
            flops=4 * count * rows * heads * HD * HD,
            bytes_accessed=4 * state.size + 4 * count * rows * heads * HD,
            transcendentals=0,
        ),
        name="read_states",
    )(*queries, state)


def where_am_i():
    return lax.axis_index("grp"), lax.axis_index("dec")


def rank_of(owner_ref, prompt):
    owner = owner_ref[prompt]
    rank = jnp.int32(0)
    for other in range(owner_ref.shape[0]):
        rank = rank + jnp.where((owner_ref[other] == owner) & (other < prompt), 1, 0)
    return owner, rank


def prompts_of(owner_ref, owner, slots):
    found = [jnp.int32(0)] * slots
    seen = jnp.int32(0)
    for prompt in range(owner_ref.shape[0]):
        mine = owner_ref[prompt] == owner
        found = [
            jnp.where(mine & (seen == slot), prompt, one) for slot, one in enumerate(found)
        ]
        seen = seen + jnp.where(mine, 1, 0)
    return found


def copy_one(choice, pool, write):
    for index, take in enumerate(pool):

        @pl.when(choice == index)
        def _(take=take):
            write(take())


def held_at(offset, near):
    spot = jnp.int32(0)
    low, high = 1, near
    while high > 1:
        spot = spot + jnp.where((offset & high) != 0, low, 0)
        low, high = low * 2, high // 2
    return spot


def one_hot(mask):
    return mask.astype(f32).astype(bf16)


def stack_rows(parts):
    return jnp.concatenate([part.astype(f32) for part in parts], axis=0)


def parcel_kernel(near, capacity, owner_ref, parent_ref, *refs):
    pool, (keys_ref, values_ref) = refs[: 2 * near], refs[2 * near : 2 * near + 2]
    outs = refs[2 * near + 2 :]
    group, block = where_am_i()
    count = len(outs)
    rows, columns = outs[0].shape
    steps, slots, per_block = keys_ref.shape[:3]
    halves = rows // (2 * capacity)
    split = columns // halves
    lines = slots * per_block
    first_keys = stack_rows([keys_ref[0, slot] for slot in range(slots)]).astype(bf16)
    first_values = stack_rows([values_ref[0, slot] for slot in range(slots)]).astype(bf16)
    for bit, out in enumerate(outs):
        owner, rank = rank_of(owner_ref, group * count + (block ^ bit))
        offset = owner ^ group
        choice = held_at(offset, near) + jnp.where((offset & 1) != 0, near, 0)

        def write(value, out=out):
            out[:, :columns] = stack_rows(value).astype(bf16)

        copy_one(
            choice,
            [
                lambda ref=ref, rank=rank: [ref[step, rank] for step in range(steps)]
                for ref in pool
            ],
            write,
        )
        if bit == 0:
            continue
        target = block ^ bit
        seen = jnp.int32(0)
        sources = [jnp.int32(0)] * capacity
        for slot in range(slots):
            for beam in range(per_block):
                parent = parent_ref[slot, target * per_block + beam]
                hit = lax.div(parent, per_block) == block
                row = slot * per_block + parent - block * per_block
                sources = [
                    jnp.where(hit & (seen == index), row, one)
                    for index, one in enumerate(sources)
                ]
                seen = seen + jnp.where(hit, 1, 0)
        line, source = iota((rows, lines), 0), iota((rows, lines), 1)
        parcel = jnp.zeros((rows, split), f32)
        for half in range(halves):
            span = slice(half * split, (half + 1) * split)
            first = half * 2 * capacity
            for kind, held in enumerate((first_keys, first_values)):
                mask = (line == first + kind * capacity) & (source == sources[0])
                for index in range(1, capacity):
                    mask = mask | (
                        (line == first + kind * capacity + index) & (source == sources[index])
                    )
                parcel = parcel + dot(one_hot(mask), held[:, span])
        out[:, columns:] = parcel.astype(bf16)


def parcels(owner, parents, pool, keys, values, capacity, count):
    whole = pl.BlockSpec(memory_space=pltpu.VMEM)
    scalar = pl.BlockSpec(memory_space=pltpu.SMEM)
    steps, _, per_block, columns = keys.shape
    rows = steps * per_block
    wide = columns + columns * 2 * capacity // rows
    return pl.pallas_call(
        functools.partial(parcel_kernel, len(pool) // 2, capacity),
        in_specs=[scalar] * 2 + [whole] * (len(pool) + 2),
        out_specs=[whole] * count,
        out_shape=[
            jax.ShapeDtypeStruct((rows, wide if bit else columns), bf16) for bit in range(count)
        ],
        compiler_params=pltpu.CompilerParams(vmem_limit_bytes=12 * MIB),
        name="parcels",
    )(owner, parents, *pool, keys, values)


def reply_kernel(near, owner_ref, *refs):
    pool, out_ref = refs[:-1], refs[-1]
    group, block = where_am_i()
    count = len(pool) // near
    for slot, prompt in enumerate(prompts_of(owner_ref, group ^ 1, out_ref.shape[0])):
        offset = lax.div(prompt, count) ^ group
        choice = held_at(offset, near) * count + (lax.rem(prompt, count) ^ block)

        def write(value, slot=slot):
            out_ref[slot] = value

        copy_one(choice, [lambda ref=ref: ref[...] for ref in pool], write)


def reply(owner, pool, near, slots):
    whole = pl.BlockSpec(memory_space=pltpu.VMEM)
    scalar = pl.BlockSpec(memory_space=pltpu.SMEM)
    return pl.pallas_call(
        functools.partial(reply_kernel, near),
        in_specs=[scalar] + [whole] * len(pool),
        out_specs=whole,
        out_shape=jax.ShapeDtypeStruct((slots,) + pool[0].shape, bf16),
        compiler_params=pltpu.CompilerParams(vmem_limit_bytes=8 * MIB),
        name="reply",
    )(owner, *pool)


def terms_kernel(capacity, count, parent_ref, decay_ref, queries_ref, keys_ref, values_ref, *refs):
    far = refs[:count]
    terms_ref, first_ref, second, parent_keys, parent_values = refs[count + 1 :]
    block = where_am_i()[1]
    steps, slots, per_block, columns = queries_ref.shape
    heads = columns // HD
    rows = steps * per_block
    lines = slots * rows
    halves = rows // (2 * capacity)
    split = columns // halves
    line = iota((lines, LANES), 0)
    near_col = jnp.full((lines, LANES), -1, jnp.int32)
    far_col = jnp.full((lines, LANES), -1, jnp.int32)
    sources = []
    for slot in range(slots):
        for beam in range(per_block):
            parent = parent_ref[slot, block * per_block + beam]
            source = lax.div(parent, per_block)
            rank = jnp.int32(0)
            for other in sources:
                rank = rank + jnp.where(other == source, 1, 0)
            sources.append(source)
            away = source ^ block
            near_at = slot * per_block + parent - source * per_block
            near_at = jnp.where(away == 0, near_at, -1)
            far_at = jnp.where(away == 0, -1, (away - 1) * rows + rank)
            here = line == slot * rows + per_block + beam
            near_col = jnp.where(here, near_at, near_col)
            far_col = jnp.where(here, far_at, far_col)
            own = block * per_block + beam
            now = slot * rows + beam
            then = now + per_block
            step_one = decay_ref[1, slot, pl.ds(own, 1), :]
            first_ref[now : now + 1, :] = decay_ref[0, slot, pl.ds(own, 1), :]
            first_ref[then : then + 1, :] = step_one + decay_ref[0, slot, pl.ds(parent, 1), :]
            second[now : now + 1, :] = jnp.full_like(step_one, -1e30)
            second[then : then + 1, :] = step_one
    first_ref[...] = jnp.exp(first_ref[...])
    second[...] = jnp.exp(second[...])
    held = slots * per_block
    own_hot = one_hot(iota((lines, held), 1) == near_col[:, :held])
    column = iota((lines, rows), 1)
    for half in range(halves):
        span = slice(half * split, (half + 1) * split)
        for kind, (ref, store) in enumerate(
            ((keys_ref, parent_keys), (values_ref, parent_values))
        ):
            own = stack_rows([ref[0, slot, :, span] for slot in range(slots)])
            picked = dot(own_hot, own.astype(bf16))
            for index, message in enumerate(far):
                low, high = half * 2 * capacity, kind * capacity
                hot = (column == far_col[:, :rows] - index * rows + low + high) & (
                    (far_col[:, :rows] >= index * rows)
                    & (far_col[:, :rows] < index * rows + capacity)
                )
                picked = picked + dot(one_hot(hot), message[:, columns:])
            store[:, span] = picked
    for head in range(heads):
        span = slice(head * HD, (head + 1) * HD)
        queries, keys, values = [
            stack_rows([ref[step, slot, :, span] for slot in range(slots) for step in range(steps)])
            for ref in (queries_ref, keys_ref, values_ref)
        ]
        own = jnp.sum(queries * keys, axis=1, keepdims=True)
        parent = jnp.sum(queries * parent_keys[:, span], axis=1, keepdims=True)
        terms_ref[:, span] = own * values + (
            second[:, head : head + 1] * parent
        ) * parent_values[:, span]


def step_terms(parents, decay, queries, keys, values, far, capacity, after):
    steps, slots, per_block, columns = queries.shape
    lines = steps * slots * per_block
    heads = columns // HD
    whole = pl.BlockSpec(memory_space=pltpu.VMEM)
    scalar = pl.BlockSpec(memory_space=pltpu.SMEM)
    return pl.pallas_call(
        functools.partial(terms_kernel, capacity, len(far)),
        in_specs=[scalar]
        + [whole] * (4 + len(far))
        + [pl.BlockSpec(memory_space=pl.ANY)],
        out_shape=[
            jax.ShapeDtypeStruct((lines, columns), f32),
            jax.ShapeDtypeStruct((lines, heads), f32),
        ],
        scratch_shapes=[
            pltpu.VMEM((lines, heads), f32),
            pltpu.VMEM((lines, columns), f32),
            pltpu.VMEM((lines, columns), f32),
        ],
        compiler_params=pltpu.CompilerParams(vmem_limit_bytes=12 * MIB),
        name="step_terms",
    )(parents, decay, queries, keys, values, *far, after)


def steps_kernel(heads, near, owner_ref, *refs):
    pool = refs[:-5]
    came_ref, terms_ref, first_ref, mixed_ref, sums_ref = refs[-5:]
    group, block = where_am_i()
    count = len(pool) // near
    slots, rows = came_ref.shape[:2]
    for slot, prompt in enumerate(prompts_of(owner_ref, group, slots)):
        offset = lax.div(prompt, count) ^ group
        choice = held_at(offset, near) * count + (lax.rem(prompt, count) ^ block)
        choice = jnp.where((offset & 1) != 0, len(pool), choice)
        lines = slice(slot * rows, (slot + 1) * rows)
        total = jnp.zeros((rows, HD), f32)
        for head in range(heads):
            span = slice(head * HD, (head + 1) * HD)
            read = came_ref[slot, :, span].astype(f32)
            for index in range(len(pool)):
                read = jnp.where(choice == index, pool[index][:, span].astype(f32), read)
            mixed = first_ref[lines, head : head + 1] * read + terms_ref[lines, span]
            mixed_ref[lines, span] = mixed
            total = total + mixed * mixed
        sums_ref[lines, :] = jnp.broadcast_to(
            jnp.sum(total, axis=1, keepdims=True), (rows, LANES)
        )


def steps_mix(owner, pool, near, came, terms, first):
    lines, columns = terms.shape
    whole = pl.BlockSpec(memory_space=pltpu.VMEM)
    scalar = pl.BlockSpec(memory_space=pltpu.SMEM)
    return pl.pallas_call(
        functools.partial(steps_kernel, columns // HD, near),
        in_specs=[scalar] + [whole] * (len(pool) + 3),
        out_shape=[
            jax.ShapeDtypeStruct((lines, columns), f32),
            jax.ShapeDtypeStruct((lines, LANES), f32),
        ],
        compiler_params=pltpu.CompilerParams(vmem_limit_bytes=12 * MIB),
        name="steps_mix",
    )(owner, *pool, came, terms, first)


def finish_kernel(width, count, gain_ref, mixed_ref, *refs):
    out_ref = refs[count]
    steps, slots, per_block, columns = out_ref.shape
    total = refs[0][...]
    for ref in refs[1:count]:
        total = total + ref[...]
    scale = lax.rsqrt(total * (1.0 / width) + epsilon)
    for column in range(0, columns, LANES):
        span = slice(column, column + LANES)
        scaled = (mixed_ref[:, span] * scale * gain_ref[:, span]).astype(bf16)
        for slot in range(slots):
            for step in range(steps):
                line = (slot * steps + step) * per_block
                out_ref[step, slot, :, span] = scaled[line : line + per_block]


def finish(gain, mixed, sums, shape):
    whole = pl.BlockSpec(memory_space=pltpu.VMEM)
    return pl.pallas_call(
        functools.partial(finish_kernel, HEAD_COUNT * HD, len(sums)),
        in_specs=[whole] * (2 + len(sums)),
        out_shape=jax.ShapeDtypeStruct(shape, bf16),
        compiler_params=pltpu.CompilerParams(vmem_limit_bytes=8 * MIB),
        name="finish",
    )(gain, mixed, *sums)


def swap(array, axis, bit):
    size = lax.axis_size(axis)
    return lax.ppermute(array, axis, [(index, index ^ bit) for index in range(size)])


def exchange(parts):
    order = sorted(range(1, len(parts)), key=lambda bit: (bit & 1, bit))
    came = {bit: swap(parts[bit], "dec", bit) for bit in order}
    return [came[bit] for bit in range(1, len(parts))]


def over_pre(array):
    size = lax.axis_size("pre")
    return [array] + [swap(array, "pre", bit) for bit in range(1, size)]


def local(
    prompt_queries,
    prompt_keys,
    prompt_values,
    prompt_decay,
    prompt_lengths,
    norm_gain,
    decode_owner,
    parent_beam,
    step_queries,
    step_keys,
    step_values,
    step_decay,
):
    tokens, columns = prompt_queries.shape[1:]
    slots = step_queries.shape[1]
    group_count, block_count = lax.axis_size("grp"), lax.axis_size("dec")
    near = group_count // 2
    capacity = (slots + block_count - 2) // (block_count - 1)
    gain = norm_gain[None]

    def widen(pool):
        bit = near
        while bit > 1:
            pool = pool + [swap(one, "grp", bit) for one in pool]
            bit //= 2
        return pool

    asked = widen([step_queries])
    sibling = swap(step_queries, "grp", 1)
    mixed, sums, state = prompt_pass(
        prompt_lengths, prompt_decay[0], prompt_queries[0], prompt_keys[0], prompt_values[0], sibling
    )
    far_rows, sums = lax.optimization_barrier((asked[1:], sums))
    asked = [step_queries] + far_rows + [sibling] + [swap(one, "grp", 1) for one in far_rows]

    messages = parcels(
        decode_owner, parent_beam, asked, step_keys, step_values, capacity, block_count
    )
    far = exchange(messages)
    squares = over_pre(sums)
    share = tokens // 4

    def norm(first, count, out, after, **more):
        return prompt_norm(
            prompt_lengths,
            gain,
            mixed,
            squares,
            first * share,
            count * share,
            out,
            after,
            **more,
        )

    prompt_out = norm(0, 1, None, messages[-1])
    state, prompt_out = lax.optimization_barrier((state, prompt_out))
    reads = read_states([messages[0]] + far, state)
    prompt_out = norm(1, 2, prompt_out, reads[-1])
    replies = exchange(reads)
    early = widen([reads[0]])
    replies, prompt_out = lax.optimization_barrier((replies, prompt_out))
    prompt_out = norm(3, 1, prompt_out, replies[-1], room=12)
    late = widen(replies)
    spread = len(early)
    pool = []
    for index in range(spread):
        pool = pool + [early[index]] + late[index * len(replies) : (index + 1) * len(replies)]
    terms, first = step_terms(
        parent_beam, step_decay, step_queries, step_keys, step_values, far, capacity, replies[-1]
    )
    pool, terms, prompt_out = lax.optimization_barrier((pool, terms, prompt_out))
    sent = reply(decode_owner, pool, near, slots)
    came = swap(sent, "grp", 1)
    step_mixed, step_sums = steps_mix(decode_owner, pool, near, came, terms, first)
    step_out = finish(gain, step_mixed, over_pre(step_sums), step_queries.shape)
    return (prompt_out[None], step_out)


def solution(mesh):
    in_specs = (
        P(("grp", "dec"), None, "pre"),
        P(("grp", "dec"), None, "pre"),
        P(("grp", "dec"), None, "pre"),
        P(("grp", "dec"), "pre", None),
        P(("grp", "dec")),
        P("pre"),
        P(),
        P("grp", None),
        P(None, "grp", "dec", "pre"),
        P(None, "grp", "dec", "pre"),
        P(None, "grp", "dec", "pre"),
        P(None, "grp", None, "pre"),
    )
    out_specs = (P(("grp", "dec"), None, "pre"), P(None, "grp", "dec", "pre"))
    return jax.shard_map(local, mesh=mesh, in_specs=in_specs, out_specs=out_specs, check_vma=False)
```

```python
import functools
import math

import jax
import jax.numpy as jnp
from jax import lax
from jax.experimental import pallas as pl
from jax.experimental.pallas import tpu as pltpu
from jax.sharding import PartitionSpec as P

HEAD_COUNT = 64
HD = 128
SUB = 128
LANES = 128
LOG2E = math.log2(math.e)
MIB = 1024 * 1024

highest = lax.Precision.HIGHEST
epsilon = 1e-06
f32 = jnp.float32
bf16 = jnp.bfloat16


def dot_nt(left, right, **more):
    return lax.dot_general(
        left, right, (((1,), (1,)), ((), ())), preferred_element_type=f32, **more
    )


def dot_tn(left, right):
    return lax.dot_general(left, right, (((0,), (0,)), ((), ())), preferred_element_type=f32)


def iota(shape, dim):
    return lax.broadcasted_iota(jnp.int32, shape, dim)


def pieces(array, count):
    parts = []
    for _ in range(count):
        part = array.astype(bf16)
        parts.append(part)
        array = array - part.astype(f32)
    return parts


def dot(left, right):
    return jnp.dot(left, right, preferred_element_type=f32)


def pass_kernel(heads, subs, each, length_ref, decay_ref, queries_ref, keys_ref, values_ref, after_ref, mixed_ref, sums_ref, state_ref, fade, lift, keep, total):
    step = pl.program_id(0)
    lower = iota((SUB, SUB), 1) <= iota((SUB, SUB), 0)

    @pl.when(step == 0)
    def _():
        upper = iota((SUB, SUB), 0) <= iota((SUB, SUB), 1)
        upper = upper.astype(f32).astype(bf16)
        earlier = lower.astype(f32).astype(bf16)
        rates, live = [], []
        for sub in range(subs):
            span = slice(sub * SUB, (sub + 1) * SUB)
            alive = sub * SUB + iota((heads, SUB), 1) < length_ref[0]
            rates.append(jnp.where(alive, decay_ref[:, span] * LOG2E, 0.0))
            live.append(alive)
        rates = jnp.concatenate(pieces(jnp.concatenate(rates, axis=0), 3), axis=1)
        row = dot(rates, jnp.concatenate([upper] * 3, axis=0))
        col = dot_nt(jnp.concatenate([earlier] * 3, axis=1), rates)
        half = 0.5 * row[:, SUB - 1 : SUB]
        fall = jnp.exp2(half - row)
        rise = jnp.exp2(col - 0.5 * col[SUB - 1 : SUB, :])
        scale = jnp.exp2(half)
        for sub in range(subs):
            span = slice(sub * heads, (sub + 1) * heads)
            fade[sub] = jnp.where(live[sub], fall[span], 0.0)
            lift[sub, :, :heads] = rise[:, span]
            after = scale[(sub + 1) * heads : (sub + 2) * heads] if sub + 1 < subs else 1.0
            keep[sub] = jnp.broadcast_to(scale[span] * after, (heads, LANES))
        state_ref[...] = jnp.zeros_like(state_ref)

    for index in range(each):
        sub = step * each + index
        rows = slice(index * SUB, (index + 1) * SUB)
        acc = jnp.zeros((SUB, HD), f32)
        for head in range(heads):
            span = slice(head * HD, (head + 1) * HD)
            queries = queries_ref[rows, span]
            values = values_ref[rows, span]
            keys = jnp.transpose(keys_ref[rows, span])
            weight = fade[sub, head : head + 1, :]
            faded = (keys.astype(f32) * weight).astype(bf16)
            scores = jnp.where(lower, dot(queries, keys) * weight, 0.0).astype(bf16)
            state = state_ref[head]
            mixed = dot(
                jnp.concatenate([scores, queries], axis=1),
                jnp.concatenate([values, state.astype(bf16)], axis=0),
            )
            mixed = mixed * lift[sub, :, head : head + 1]
            state_ref[head] = (state + dot(faded, values)) * keep[sub, head : head + 1, :]
            mixed_ref[rows, span] = mixed.astype(bf16)
            acc = acc + mixed * mixed
        total[pl.ds(pl.multiple_of(sub * SUB, SUB), SUB), :] = acc

    @pl.when(step == subs // each - 1)
    def _():
        sums_ref[...] = dot_nt(
            jnp.ones((8, 2 * HD), bf16), jnp.concatenate(pieces(total[...], 2), axis=1)
        )


def prompt_pass(lengths, decay, queries, keys, values, after):
    heads, tokens = decay.shape
    columns = heads * HD
    subs = tokens // SUB
    each = 2
    wide = pl.BlockSpec((SUB * each, columns), lambda b: (b, 0))
    return pl.pallas_call(
        functools.partial(pass_kernel, heads, subs, each),
        grid=(subs // each,),
        in_specs=[
            pl.BlockSpec(memory_space=pltpu.SMEM),
            pl.BlockSpec((heads, tokens), lambda b: (0, 0)),
            wide,
            wide,
            wide,
            pl.BlockSpec(memory_space=pl.ANY),
        ],
        out_specs=[
            wide,
            pl.BlockSpec((8, tokens), lambda b: (0, 0)),
            pl.BlockSpec((heads, HD, HD), lambda b: (0, 0, 0)),
        ],
        out_shape=[
            jax.ShapeDtypeStruct((tokens, columns), bf16),
            jax.ShapeDtypeStruct((8, tokens), f32),
            jax.ShapeDtypeStruct((heads, HD, HD), f32),
        ],
        scratch_shapes=[
            pltpu.VMEM((subs, heads, LANES), f32),
            pltpu.VMEM((subs, SUB, LANES), f32),
            pltpu.VMEM((subs, heads, LANES), f32),
            pltpu.VMEM((tokens, HD), f32),
        ],
        compiler_params=pltpu.CompilerParams(vmem_limit_bytes=40 * MIB),
        cost_estimate=pl.CostEstimate(
            flops=8 * tokens * columns * HD, bytes_accessed=8 * tokens * columns, transcendentals=0
        ),
        name="prompt_pass",
    )(lengths, decay, queries, keys, values, after)


def norm_kernel(width, count, base, length_ref, gain_ref, mixed_ref, *refs):
    block = pl.program_id(0)
    out_ref = refs[-1]
    total = refs[0][...]
    for ref in refs[1:count]:
        total = total + ref[...]
    scale = lax.rsqrt(total * (1.0 / width) + epsilon)
    rows = scale.shape[1]
    scale = jnp.where(base + block * rows + iota(scale.shape, 1) < length_ref[0], scale, 0.0)
    scale = jnp.transpose(scale)[:, :1]
    for column in range(0, gain_ref.shape[1], 512):
        span = slice(column, column + 512)
        out_ref[:, span] = (
            mixed_ref[:, span].astype(f32) * scale * gain_ref[:, span]
        ).astype(bf16)


def prompt_norm(lengths, gain, mixed, sums, base, rows, out, after, room=12, lines=SUB):
    tokens, columns = mixed.shape
    skip = base // lines
    spare = pl.BlockSpec(memory_space=pl.ANY)
    more = [after] if out is None else [after, out]
    return pl.pallas_call(
        functools.partial(norm_kernel, HEAD_COUNT * HD, len(sums), base),
        grid=(rows // lines,),
        in_specs=[
            pl.BlockSpec(memory_space=pltpu.SMEM),
            pl.BlockSpec((1, columns), lambda b: (0, 0)),
            pl.BlockSpec((lines, columns), lambda b: (b + skip, 0)),
        ]
        + [pl.BlockSpec((8, lines), lambda b: (0, b + skip))] * len(sums)
        + [spare] * len(more),
        out_specs=pl.BlockSpec((lines, columns), lambda b: (b + skip, 0)),
        out_shape=jax.ShapeDtypeStruct((tokens, columns), bf16),
        input_output_aliases={} if out is None else {4 + len(sums): 0},
        compiler_params=pltpu.CompilerParams(vmem_limit_bytes=room * MIB),
        cost_estimate=pl.CostEstimate(
            flops=3 * rows * columns, bytes_accessed=4 * rows * columns, transcendentals=0
        ),
        name="prompt_norm",
    )(lengths, gain, mixed, *sums, *more)


def read_kernel(heads, count, *refs):
    state_ref = refs[count]
    outs = refs[count + 1 :]
    rows = refs[0].shape[0]
    for head in range(heads):
        span = slice(head * HD, (head + 1) * HD)
        high, low = pieces(state_ref[head], 2)
        queries = jnp.concatenate([ref[:, span].astype(f32) for ref in refs[:count]], axis=0)
        queries = queries.astype(bf16)
        read = dot(
            jnp.concatenate([queries, queries], axis=1), jnp.concatenate([high, low], axis=0)
        )
        for index, out in enumerate(outs):
            out[:, span] = read[index * rows : (index + 1) * rows].astype(bf16)


def read_states(queries, state):
    heads = state.shape[0]
    count = len(queries)
    rows = queries[0].shape[0]
    group = min(8, heads)
    part = pl.BlockSpec((rows, group * HD), lambda g: (0, g))
    return pl.pallas_call(
        functools.partial(read_kernel, group, count),
        grid=(heads // group,),
        in_specs=[part] * count + [pl.BlockSpec((group, HD, HD), lambda g: (g, 0, 0))],
        out_specs=[part] * count,
        out_shape=[jax.ShapeDtypeStruct((rows, heads * HD), bf16)] * count,
        compiler_params=pltpu.CompilerParams(vmem_limit_bytes=12 * MIB),
        cost_estimate=pl.CostEstimate(
            flops=4 * count * rows * heads * HD * HD,
            bytes_accessed=4 * state.size + 4 * count * rows * heads * HD,
            transcendentals=0,
        ),
        name="read_states",
    )(*queries, state)


def where_am_i():
    return lax.axis_index("grp"), lax.axis_index("dec")


def rank_of(owner_ref, prompt):
    owner = owner_ref[prompt]
    rank = jnp.int32(0)
    for other in range(owner_ref.shape[0]):
        rank = rank + jnp.where((owner_ref[other] == owner) & (other < prompt), 1, 0)
    return owner, rank


def prompts_of(owner_ref, owner, slots):
    found = [jnp.int32(0)] * slots
    seen = jnp.int32(0)
    for prompt in range(owner_ref.shape[0]):
        mine = owner_ref[prompt] == owner
        found = [
            jnp.where(mine & (seen == slot), prompt, one) for slot, one in enumerate(found)
        ]
        seen = seen + jnp.where(mine, 1, 0)
    return found


def copy_one(choice, pool, write):
    for index, take in enumerate(pool):

        @pl.when(choice == index)
        def _(take=take):
            write(take())


def held_at(offset, near):
    spot = jnp.int32(0)
    low, high = 1, near
    while high > 1:
        spot = spot + jnp.where((offset & high) != 0, low, 0)
        low, high = low * 2, high // 2
    return spot


def one_hot(mask):
    return mask.astype(f32).astype(bf16)


def stack_rows(parts):
    return jnp.concatenate([part.astype(f32) for part in parts], axis=0)


def parcel_kernel(near, capacity, owner_ref, parent_ref, *refs):
    pool, (keys_ref, values_ref) = refs[: 2 * near], refs[2 * near : 2 * near + 2]
    outs = refs[2 * near + 2 :]
    group, block = where_am_i()
    count = len(outs)
    rows, columns = outs[0].shape
    steps, slots, per_block = keys_ref.shape[:3]
    halves = rows // (2 * capacity)
    split = columns // halves
    lines = slots * per_block
    first_keys = stack_rows([keys_ref[0, slot] for slot in range(slots)]).astype(bf16)
    first_values = stack_rows([values_ref[0, slot] for slot in range(slots)]).astype(bf16)
    for bit, out in enumerate(outs):
        owner, rank = rank_of(owner_ref, group * count + (block ^ bit))
        offset = owner ^ group
        choice = held_at(offset, near) + jnp.where((offset & 1) != 0, near, 0)

        def write(value, out=out):
            out[:, :columns] = stack_rows(value).astype(bf16)

        copy_one(
            choice,
            [
                lambda ref=ref, rank=rank: [ref[step, rank] for step in range(steps)]
                for ref in pool
            ],
            write,
        )
        if bit == 0:
            continue
        target = block ^ bit
        seen = jnp.int32(0)
        sources = [jnp.int32(0)] * capacity
        for slot in range(slots):
            for beam in range(per_block):
                parent = parent_ref[slot, target * per_block + beam]
                hit = lax.div(parent, per_block) == block
                row = slot * per_block + parent - block * per_block
                sources = [
                    jnp.where(hit & (seen == index), row, one)
                    for index, one in enumerate(sources)
                ]
                seen = seen + jnp.where(hit, 1, 0)
        line, source = iota((rows, lines), 0), iota((rows, lines), 1)
        parcel = jnp.zeros((rows, split), f32)
        for half in range(halves):
            span = slice(half * split, (half + 1) * split)
            first = half * 2 * capacity
            for kind, held in enumerate((first_keys, first_values)):
                mask = (line == first + kind * capacity) & (source == sources[0])
                for index in range(1, capacity):
                    mask = mask | (
                        (line == first + kind * capacity + index) & (source == sources[index])
                    )
                parcel = parcel + dot(one_hot(mask), held[:, span])
        out[:, columns:] = parcel.astype(bf16)


def parcels(owner, parents, pool, keys, values, capacity, count):
    whole = pl.BlockSpec(memory_space=pltpu.VMEM)
    scalar = pl.BlockSpec(memory_space=pltpu.SMEM)
    steps, _, per_block, columns = keys.shape
    rows = steps * per_block
    wide = columns + columns * 2 * capacity // rows
    return pl.pallas_call(
        functools.partial(parcel_kernel, len(pool) // 2, capacity),
        in_specs=[scalar] * 2 + [whole] * (len(pool) + 2),
        out_specs=[whole] * count,
        out_shape=[
            jax.ShapeDtypeStruct((rows, wide if bit else columns), bf16) for bit in range(count)
        ],
        compiler_params=pltpu.CompilerParams(vmem_limit_bytes=12 * MIB),
        name="parcels",
    )(owner, parents, *pool, keys, values)


def reply_kernel(near, owner_ref, *refs):
    pool, out_ref = refs[:-1], refs[-1]
    group, block = where_am_i()
    count = len(pool) // near
    for slot, prompt in enumerate(prompts_of(owner_ref, group ^ 1, out_ref.shape[0])):
        offset = lax.div(prompt, count) ^ group
        choice = held_at(offset, near) * count + (lax.rem(prompt, count) ^ block)

        def write(value, slot=slot):
            out_ref[slot] = value

        copy_one(choice, [lambda ref=ref: ref[...] for ref in pool], write)


def reply(owner, pool, near, slots):
    whole = pl.BlockSpec(memory_space=pltpu.VMEM)
    scalar = pl.BlockSpec(memory_space=pltpu.SMEM)
    return pl.pallas_call(
        functools.partial(reply_kernel, near),
        in_specs=[scalar] + [whole] * len(pool),
        out_specs=whole,
        out_shape=jax.ShapeDtypeStruct((slots,) + pool[0].shape, bf16),
        compiler_params=pltpu.CompilerParams(vmem_limit_bytes=8 * MIB),
        name="reply",
    )(owner, *pool)


def lane_sum(array):
    halves = jnp.concatenate(pieces(array, 2), axis=1)
    return dot(halves, jnp.ones((2 * HD, HD), bf16))


def terms_kernel(capacity, count, parent_ref, decay_ref, queries_ref, keys_ref, values_ref, *refs):
    far = refs[:count]
    terms_ref, first_ref, second, parent_keys, parent_values = refs[count + 1 :]
    block = where_am_i()[1]
    steps, slots, per_block, columns = queries_ref.shape
    heads = columns // HD
    rows = steps * per_block
    lines = slots * rows
    halves = rows // (2 * capacity)
    split = columns // halves
    line = iota((lines, LANES), 0)
    near_col = jnp.full((lines, LANES), -1, jnp.int32)
    far_col = jnp.full((lines, LANES), -1, jnp.int32)
    sources = []
    for slot in range(slots):
        for beam in range(per_block):
            parent = parent_ref[slot, block * per_block + beam]
            source = lax.div(parent, per_block)
            rank = jnp.int32(0)
            for other in sources:
                rank = rank + jnp.where(other == source, 1, 0)
            sources.append(source)
            away = source ^ block
            near_at = slot * per_block + parent - source * per_block
            near_at = jnp.where(away == 0, near_at, -1)
            far_at = jnp.where(away == 0, -1, (away - 1) * rows + rank)
            here = line == slot * rows + per_block + beam
            near_col = jnp.where(here, near_at, near_col)
            far_col = jnp.where(here, far_at, far_col)
            own = block * per_block + beam
            now = slot * rows + beam
            then = now + per_block
            step_one = decay_ref[1, slot, pl.ds(own, 1), :]
            first_ref[now : now + 1, :] = decay_ref[0, slot, pl.ds(own, 1), :]
            first_ref[then : then + 1, :] = step_one + decay_ref[0, slot, pl.ds(parent, 1), :]
            second[now : now + 1, :] = jnp.full_like(step_one, -1e30)
            second[then : then + 1, :] = step_one
    first_ref[...] = jnp.exp(first_ref[...])
    second[...] = jnp.exp(second[...])
    held = slots * per_block
    own_hot = one_hot(iota((lines, held), 1) == near_col[:, :held])
    column = iota((lines, rows), 1)
    for half in range(halves):
        span = slice(half * split, (half + 1) * split)
        for kind, (ref, store) in enumerate(
            ((keys_ref, parent_keys), (values_ref, parent_values))
        ):
            own = stack_rows([ref[0, slot, :, span] for slot in range(slots)])
            picked = dot(own_hot, own.astype(bf16))
            for index, message in enumerate(far):
                low, high = half * 2 * capacity, kind * capacity
                hot = (column == far_col[:, :rows] - index * rows + low + high) & (
                    (far_col[:, :rows] >= index * rows)
                    & (far_col[:, :rows] < index * rows + capacity)
                )
                picked = picked + dot(one_hot(hot), message[:, columns:])
            store[:, span] = picked
    for head in range(heads):
        span = slice(head * HD, (head + 1) * HD)
        queries, keys, values = [
            stack_rows([ref[step, slot, :, span] for slot in range(slots) for step in range(steps)])
            for ref in (queries_ref, keys_ref, values_ref)
        ]
        own = lane_sum(queries * keys)
        parent = lane_sum(queries * parent_keys[:, span])
        terms_ref[:, span] = own * values + (
            second[:, head : head + 1] * parent
        ) * parent_values[:, span]


def step_terms(parents, decay, queries, keys, values, far, capacity, after):
    steps, slots, per_block, columns = queries.shape
    lines = steps * slots * per_block
    heads = columns // HD
    whole = pl.BlockSpec(memory_space=pltpu.VMEM)
    scalar = pl.BlockSpec(memory_space=pltpu.SMEM)
    return pl.pallas_call(
        functools.partial(terms_kernel, capacity, len(far)),
        in_specs=[scalar]
        + [whole] * (4 + len(far))
        + [pl.BlockSpec(memory_space=pl.ANY)],
        out_shape=[
            jax.ShapeDtypeStruct((lines, columns), f32),
            jax.ShapeDtypeStruct((lines, heads), f32),
        ],
        scratch_shapes=[
            pltpu.VMEM((lines, heads), f32),
            pltpu.VMEM((lines, columns), f32),
            pltpu.VMEM((lines, columns), f32),
        ],
        compiler_params=pltpu.CompilerParams(vmem_limit_bytes=12 * MIB),
        name="step_terms",
    )(parents, decay, queries, keys, values, *far, after)


def steps_kernel(heads, near, owner_ref, *refs):
    pool = refs[:-5]
    came_ref, terms_ref, first_ref, mixed_ref, sums_ref = refs[-5:]
    group, block = where_am_i()
    count = len(pool) // near
    slots, rows = came_ref.shape[:2]
    for slot, prompt in enumerate(prompts_of(owner_ref, group, slots)):
        offset = lax.div(prompt, count) ^ group
        choice = held_at(offset, near) * count + (lax.rem(prompt, count) ^ block)
        choice = jnp.where((offset & 1) != 0, len(pool), choice)
        lines = slice(slot * rows, (slot + 1) * rows)
        total = jnp.zeros((rows, HD), f32)
        for head in range(heads):
            span = slice(head * HD, (head + 1) * HD)
            read = came_ref[slot, :, span].astype(f32)
            for index in range(len(pool)):
                read = jnp.where(choice == index, pool[index][:, span].astype(f32), read)
            mixed = first_ref[lines, head : head + 1] * read + terms_ref[lines, span]
            mixed_ref[lines, span] = mixed
            total = total + mixed * mixed
        sums_ref[lines, :] = jnp.broadcast_to(
            jnp.sum(total, axis=1, keepdims=True), (rows, LANES)
        )


def steps_mix(owner, pool, near, came, terms, first):
    lines, columns = terms.shape
    whole = pl.BlockSpec(memory_space=pltpu.VMEM)
    scalar = pl.BlockSpec(memory_space=pltpu.SMEM)
    return pl.pallas_call(
        functools.partial(steps_kernel, columns // HD, near),
        in_specs=[scalar] + [whole] * (len(pool) + 3),
        out_shape=[
            jax.ShapeDtypeStruct((lines, columns), f32),
            jax.ShapeDtypeStruct((lines, LANES), f32),
        ],
        compiler_params=pltpu.CompilerParams(vmem_limit_bytes=12 * MIB),
        name="steps_mix",
    )(owner, *pool, came, terms, first)


def finish_kernel(width, count, gain_ref, mixed_ref, *refs):
    out_ref = refs[count]
    steps, slots, per_block, columns = out_ref.shape
    total = refs[0][...]
    for ref in refs[1:count]:
        total = total + ref[...]
    scale = lax.rsqrt(total * (1.0 / width) + epsilon)
    for column in range(0, columns, LANES):
        span = slice(column, column + LANES)
        scaled = (mixed_ref[:, span] * scale * gain_ref[:, span]).astype(bf16)
        for slot in range(slots):
            for step in range(steps):
                line = (slot * steps + step) * per_block
                out_ref[step, slot, :, span] = scaled[line : line + per_block]


def finish(gain, mixed, sums, shape):
    whole = pl.BlockSpec(memory_space=pltpu.VMEM)
    return pl.pallas_call(
        functools.partial(finish_kernel, HEAD_COUNT * HD, len(sums)),
        in_specs=[whole] * (2 + len(sums)),
        out_shape=jax.ShapeDtypeStruct(shape, bf16),
        compiler_params=pltpu.CompilerParams(vmem_limit_bytes=8 * MIB),
        name="finish",
    )(gain, mixed, *sums)


def swap(array, axis, bit):
    size = lax.axis_size(axis)
    return lax.ppermute(array, axis, [(index, index ^ bit) for index in range(size)])


def exchange(parts):
    order = sorted(range(1, len(parts)), key=lambda bit: (bit & 1, bit))
    came = {bit: swap(parts[bit], "dec", bit) for bit in order}
    return [came[bit] for bit in range(1, len(parts))]


def over_pre(array):
    size = lax.axis_size("pre")
    return [array] + [swap(array, "pre", bit) for bit in range(1, size)]


def local(
    prompt_queries,
    prompt_keys,
    prompt_values,
    prompt_decay,
    prompt_lengths,
    norm_gain,
    decode_owner,
    parent_beam,
    step_queries,
    step_keys,
    step_values,
    step_decay,
):
    tokens, columns = prompt_queries.shape[1:]
    slots = step_queries.shape[1]
    group_count, block_count = lax.axis_size("grp"), lax.axis_size("dec")
    near = group_count // 2
    capacity = (slots + block_count - 2) // (block_count - 1)
    gain = norm_gain[None]

    def widen(pool):
        bit = near
        while bit > 1:
            pool = pool + [swap(one, "grp", bit) for one in pool]
            bit //= 2
        return pool

    asked = widen([step_queries])
    sibling = swap(step_queries, "grp", 1)
    mixed, sums, state = prompt_pass(
        prompt_lengths, prompt_decay[0], prompt_queries[0], prompt_keys[0], prompt_values[0], sibling
    )
    far_rows, sums = lax.optimization_barrier((asked[1:], sums))
    asked = [step_queries] + far_rows + [sibling] + [swap(one, "grp", 1) for one in far_rows]

    messages = parcels(
        decode_owner, parent_beam, asked, step_keys, step_values, capacity, block_count
    )
    far = exchange(messages)
    squares = over_pre(sums)
    share = tokens // 8

    def norm(first, count, out, after, **more):
        return prompt_norm(
            prompt_lengths,
            gain,
            mixed,
            squares,
            first * share,
            count * share,
            out,
            after,
            **more,
        )

    prompt_out = norm(0, 2, None, messages[-1])
    state, prompt_out = lax.optimization_barrier((state, prompt_out))
    reads = read_states([messages[0]] + far, state)
    prompt_out = norm(2, 4, prompt_out, reads[-1], lines=2 * SUB)
    replies = exchange(reads)
    early = widen([reads[0]])
    replies, prompt_out = lax.optimization_barrier((replies, prompt_out))
    late = widen(replies)
    spread = len(early)
    pool = []
    for index in range(spread):
        pool = pool + [early[index]] + late[index * len(replies) : (index + 1) * len(replies)]
    terms, first = step_terms(
        parent_beam, step_decay, step_queries, step_keys, step_values, far, capacity, replies[-1]
    )
    pool, terms, prompt_out = lax.optimization_barrier((pool, terms, prompt_out))
    sent = reply(decode_owner, pool, near, slots)
    came = swap(sent, "grp", 1)
    step_mixed, step_sums = steps_mix(decode_owner, pool, near, came, terms, first)
    step_squares = over_pre(step_sums)
    prompt_out = norm(6, 2, prompt_out, step_sums, room=12)
    step_out = finish(gain, step_mixed, step_squares, step_queries.shape)
    return (prompt_out[None], step_out)


def solution(mesh):
    in_specs = (
        P(("grp", "dec"), None, "pre"),
        P(("grp", "dec"), None, "pre"),
        P(("grp", "dec"), None, "pre"),
        P(("grp", "dec"), "pre", None),
        P(("grp", "dec")),
        P("pre"),
        P(),
        P("grp", None),
        P(None, "grp", "dec", "pre"),
        P(None, "grp", "dec", "pre"),
        P(None, "grp", "dec", "pre"),
        P(None, "grp", None, "pre"),
    )
    out_specs = (P(("grp", "dec"), None, "pre"), P(None, "grp", "dec", "pre"))
    return jax.shard_map(local, mesh=mesh, in_specs=in_specs, out_specs=out_specs, check_vma=False)
```

```python
import functools
import math

import jax
import jax.numpy as jnp
from jax import lax
from jax.experimental import pallas as pl
from jax.experimental.pallas import tpu as pltpu
from jax.sharding import PartitionSpec as P

HEAD_COUNT = 64
HD = 128
SUB = 128
LANES = 128
LOG2E = math.log2(math.e)
MIB = 1024 * 1024

highest = lax.Precision.HIGHEST
epsilon = 1e-06
f32 = jnp.float32
bf16 = jnp.bfloat16


def dot_nt(left, right, **more):
    return lax.dot_general(
        left, right, (((1,), (1,)), ((), ())), preferred_element_type=f32, **more
    )


def dot_tn(left, right):
    return lax.dot_general(left, right, (((0,), (0,)), ((), ())), preferred_element_type=f32)


def iota(shape, dim):
    return lax.broadcasted_iota(jnp.int32, shape, dim)


def pieces(array, count):
    parts = []
    for _ in range(count):
        part = array.astype(bf16)
        parts.append(part)
        array = array - part.astype(f32)
    return parts


def dot(left, right):
    return jnp.dot(left, right, preferred_element_type=f32)


def pass_kernel(heads, subs, each, length_ref, decay_ref, queries_ref, keys_ref, values_ref, after_ref, mixed_ref, sums_ref, state_ref, fade, lift, keep, total):
    step = pl.program_id(0)
    lower = iota((SUB, SUB), 1) <= iota((SUB, SUB), 0)

    @pl.when(step == 0)
    def _():
        upper = iota((SUB, SUB), 0) <= iota((SUB, SUB), 1)
        upper = upper.astype(f32).astype(bf16)
        earlier = lower.astype(f32).astype(bf16)
        rates, live = [], []
        for sub in range(subs):
            span = slice(sub * SUB, (sub + 1) * SUB)
            alive = sub * SUB + iota((heads, SUB), 1) < length_ref[...]
            rates.append(jnp.where(alive, decay_ref[:, span] * LOG2E, 0.0))
            live.append(alive)
        rates = jnp.concatenate(pieces(jnp.concatenate(rates, axis=0), 3), axis=1)
        row = dot(rates, jnp.concatenate([upper] * 3, axis=0))
        col = dot_nt(jnp.concatenate([earlier] * 3, axis=1), rates)
        half = 0.5 * row[:, SUB - 1 : SUB]
        fall = jnp.exp2(half - row)
        rise = jnp.exp2(col - 0.5 * col[SUB - 1 : SUB, :])
        scale = jnp.exp2(half)
        for sub in range(subs):
            span = slice(sub * heads, (sub + 1) * heads)
            fade[sub] = jnp.where(live[sub], fall[span], 0.0)
            lift[sub, :, :heads] = rise[:, span]
            after = scale[(sub + 1) * heads : (sub + 2) * heads] if sub + 1 < subs else 1.0
            keep[sub] = jnp.broadcast_to(scale[span] * after, (heads, LANES))
        state_ref[...] = jnp.zeros_like(state_ref)

    for index in range(each):
        sub = step * each + index
        rows = slice(index * SUB, (index + 1) * SUB)
        acc = jnp.zeros((SUB, HD), f32)
        for head in range(heads):
            span = slice(head * HD, (head + 1) * HD)
            queries = queries_ref[rows, span]
            values = values_ref[rows, span]
            keys = jnp.transpose(keys_ref[rows, span])
            weight = fade[sub, head : head + 1, :]
            faded = (keys.astype(f32) * weight).astype(bf16)
            scores = jnp.where(lower, dot(queries, keys) * weight, 0.0).astype(bf16)
            state = state_ref[head]
            mixed = dot(
                jnp.concatenate([scores, queries], axis=1),
                jnp.concatenate([values, state.astype(bf16)], axis=0),
            )
            mixed = mixed * lift[sub, :, head : head + 1]
            state_ref[head] = (state + dot(faded, values)) * keep[sub, head : head + 1, :]
            mixed_ref[rows, span] = mixed.astype(bf16)
            acc = acc + mixed * mixed
        total[pl.ds(pl.multiple_of(sub * SUB, SUB), SUB), :] = acc

    @pl.when(step == subs // each - 1)
    def _():
        sums_ref[...] = dot_nt(
            jnp.ones((8, 2 * HD), bf16), jnp.concatenate(pieces(total[...], 2), axis=1)
        )


def prompt_pass(lengths, decay, queries, keys, values, after):
    heads, tokens = decay.shape
    columns = heads * HD
    subs = tokens // SUB
    each = 2
    wide = pl.BlockSpec((SUB * each, columns), lambda b: (b, 0))
    return pl.pallas_call(
        functools.partial(pass_kernel, heads, subs, each),
        grid=(subs // each,),
        in_specs=[
            pl.BlockSpec((1, 1), lambda b: (0, 0)),
            pl.BlockSpec((heads, tokens), lambda b: (0, 0)),
            wide,
            wide,
            wide,
            pl.BlockSpec(memory_space=pl.ANY),
        ],
        out_specs=[
            wide,
            pl.BlockSpec((8, tokens), lambda b: (0, 0)),
            pl.BlockSpec((heads, HD, HD), lambda b: (0, 0, 0)),
        ],
        out_shape=[
            jax.ShapeDtypeStruct((tokens, columns), bf16),
            jax.ShapeDtypeStruct((8, tokens), f32),
            jax.ShapeDtypeStruct((heads, HD, HD), f32),
        ],
        scratch_shapes=[
            pltpu.VMEM((subs, heads, LANES), f32),
            pltpu.VMEM((subs, SUB, LANES), f32),
            pltpu.VMEM((subs, heads, LANES), f32),
            pltpu.VMEM((tokens, HD), f32),
        ],
        compiler_params=pltpu.CompilerParams(vmem_limit_bytes=40 * MIB),
        cost_estimate=pl.CostEstimate(
            flops=8 * tokens * columns * HD, bytes_accessed=8 * tokens * columns, transcendentals=0
        ),
        name="prompt_pass",
    )(lengths[None], decay, queries, keys, values, after)


def norm_kernel(width, count, base, length_ref, gain_ref, mixed_ref, *refs):
    block = pl.program_id(0)
    out_ref = refs[-1]
    total = refs[0][...]
    for ref in refs[1:count]:
        total = total + ref[...]
    scale = lax.rsqrt(total * (1.0 / width) + epsilon)
    rows = scale.shape[1]
    scale = jnp.where(base + block * rows + iota(scale.shape, 1) < length_ref[0], scale, 0.0)
    scale = jnp.transpose(scale)[:, :1]
    for column in range(0, gain_ref.shape[1], 512):
        span = slice(column, column + 512)
        out_ref[:, span] = (
            mixed_ref[:, span].astype(f32) * scale * gain_ref[:, span]
        ).astype(bf16)


def prompt_norm(lengths, gain, mixed, sums, base, rows, out, after, room=12, lines=SUB):
    tokens, columns = mixed.shape
    skip = base // lines
    spare = pl.BlockSpec(memory_space=pl.ANY)
    more = [after] if out is None else [after, out]
    return pl.pallas_call(
        functools.partial(norm_kernel, HEAD_COUNT * HD, len(sums), base),
        grid=(rows // lines,),
        in_specs=[
            pl.BlockSpec(memory_space=pltpu.SMEM),
            pl.BlockSpec((1, columns), lambda b: (0, 0)),
            pl.BlockSpec((lines, columns), lambda b: (b + skip, 0)),
        ]
        + [pl.BlockSpec((8, lines), lambda b: (0, b + skip))] * len(sums)
        + [spare] * len(more),
        out_specs=pl.BlockSpec((lines, columns), lambda b: (b + skip, 0)),
        out_shape=jax.ShapeDtypeStruct((tokens, columns), bf16),
        input_output_aliases={} if out is None else {4 + len(sums): 0},
        compiler_params=pltpu.CompilerParams(vmem_limit_bytes=room * MIB),
        cost_estimate=pl.CostEstimate(
            flops=3 * rows * columns, bytes_accessed=4 * rows * columns, transcendentals=0
        ),
        name="prompt_norm",
    )(lengths, gain, mixed, *sums, *more)


def read_kernel(heads, count, *refs):
    state_ref = refs[count]
    outs = refs[count + 1 :]
    rows = refs[0].shape[0]
    for head in range(heads):
        span = slice(head * HD, (head + 1) * HD)
        high, low = pieces(state_ref[head], 2)
        queries = jnp.concatenate([ref[:, span].astype(f32) for ref in refs[:count]], axis=0)
        queries = queries.astype(bf16)
        read = dot(
            jnp.concatenate([queries, queries], axis=1), jnp.concatenate([high, low], axis=0)
        )
        for index, out in enumerate(outs):
            out[:, span] = read[index * rows : (index + 1) * rows].astype(bf16)


def read_states(queries, state):
    heads = state.shape[0]
    count = len(queries)
    rows = queries[0].shape[0]
    group = min(8, heads)
    part = pl.BlockSpec((rows, group * HD), lambda g: (0, g))
    return pl.pallas_call(
        functools.partial(read_kernel, group, count),
        grid=(heads // group,),
        in_specs=[part] * count + [pl.BlockSpec((group, HD, HD), lambda g: (g, 0, 0))],
        out_specs=[part] * count,
        out_shape=[jax.ShapeDtypeStruct((rows, heads * HD), bf16)] * count,
        compiler_params=pltpu.CompilerParams(vmem_limit_bytes=12 * MIB),
        cost_estimate=pl.CostEstimate(
            flops=4 * count * rows * heads * HD * HD,
            bytes_accessed=4 * state.size + 4 * count * rows * heads * HD,
            transcendentals=0,
        ),
        name="read_states",
    )(*queries, state)


def where_am_i():
    return lax.axis_index("grp"), lax.axis_index("dec")


def rank_of(owner_ref, prompt):
    owner = owner_ref[prompt]
    rank = jnp.int32(0)
    for other in range(owner_ref.shape[0]):
        rank = rank + jnp.where((owner_ref[other] == owner) & (other < prompt), 1, 0)
    return owner, rank


def prompts_of(owner_ref, owner, slots):
    found = [jnp.int32(0)] * slots
    seen = jnp.int32(0)
    for prompt in range(owner_ref.shape[0]):
        mine = owner_ref[prompt] == owner
        found = [
            jnp.where(mine & (seen == slot), prompt, one) for slot, one in enumerate(found)
        ]
        seen = seen + jnp.where(mine, 1, 0)
    return found


def copy_one(choice, pool, write):
    for index, take in enumerate(pool):

        @pl.when(choice == index)
        def _(take=take):
            write(take())


def held_at(offset, near):
    spot = jnp.int32(0)
    low, high = 1, near
    while high > 1:
        spot = spot + jnp.where((offset & high) != 0, low, 0)
        low, high = low * 2, high // 2
    return spot


def one_hot(mask):
    return mask.astype(f32).astype(bf16)


def stack_rows(parts):
    return jnp.concatenate([part.astype(f32) for part in parts], axis=0)


def parcel_kernel(near, capacity, owner_ref, parent_ref, *refs):
    pool, (keys_ref, values_ref) = refs[: 2 * near], refs[2 * near : 2 * near + 2]
    outs = refs[2 * near + 2 :]
    group, block = where_am_i()
    count = len(outs)
    rows, columns = outs[0].shape
    steps, slots, per_block = keys_ref.shape[:3]
    halves = rows // (2 * capacity)
    split = columns // halves
    lines = slots * per_block
    first_keys = stack_rows([keys_ref[0, slot] for slot in range(slots)]).astype(bf16)
    first_values = stack_rows([values_ref[0, slot] for slot in range(slots)]).astype(bf16)
    for bit, out in enumerate(outs):
        owner, rank = rank_of(owner_ref, group * count + (block ^ bit))
        offset = owner ^ group
        choice = held_at(offset, near) + jnp.where((offset & 1) != 0, near, 0)

        def write(value, out=out):
            out[:, :columns] = stack_rows(value).astype(bf16)

        copy_one(
            choice,
            [
                lambda ref=ref, rank=rank: [ref[step, rank] for step in range(steps)]
                for ref in pool
            ],
            write,
        )
        if bit == 0:
            continue
        target = block ^ bit
        seen = jnp.int32(0)
        sources = [jnp.int32(0)] * capacity
        for slot in range(slots):
            for beam in range(per_block):
                parent = parent_ref[slot, target * per_block + beam]
                hit = lax.div(parent, per_block) == block
                row = slot * per_block + parent - block * per_block
                sources = [
                    jnp.where(hit & (seen == index), row, one)
                    for index, one in enumerate(sources)
                ]
                seen = seen + jnp.where(hit, 1, 0)
        line, source = iota((rows, lines), 0), iota((rows, lines), 1)
        parcel = jnp.zeros((rows, split), f32)
        for half in range(halves):
            span = slice(half * split, (half + 1) * split)
            first = half * 2 * capacity
            for kind, held in enumerate((first_keys, first_values)):
                mask = (line == first + kind * capacity) & (source == sources[0])
                for index in range(1, capacity):
                    mask = mask | (
                        (line == first + kind * capacity + index) & (source == sources[index])
                    )
                parcel = parcel + dot(one_hot(mask), held[:, span])
        out[:, columns:] = parcel.astype(bf16)


def parcels(owner, parents, pool, keys, values, capacity, count):
    whole = pl.BlockSpec(memory_space=pltpu.VMEM)
    scalar = pl.BlockSpec(memory_space=pltpu.SMEM)
    steps, _, per_block, columns = keys.shape
    rows = steps * per_block
    wide = columns + columns * 2 * capacity // rows
    return pl.pallas_call(
        functools.partial(parcel_kernel, len(pool) // 2, capacity),
        in_specs=[scalar] * 2 + [whole] * (len(pool) + 2),
        out_specs=[whole] * count,
        out_shape=[
            jax.ShapeDtypeStruct((rows, wide if bit else columns), bf16) for bit in range(count)
        ],
        compiler_params=pltpu.CompilerParams(vmem_limit_bytes=12 * MIB),
        name="parcels",
    )(owner, parents, *pool, keys, values)


def reply_kernel(near, owner_ref, *refs):
    pool, out_ref = refs[:-1], refs[-1]
    group, block = where_am_i()
    count = len(pool) // near
    for slot, prompt in enumerate(prompts_of(owner_ref, group ^ 1, out_ref.shape[0])):
        offset = lax.div(prompt, count) ^ group
        choice = held_at(offset, near) * count + (lax.rem(prompt, count) ^ block)

        def write(value, slot=slot):
            out_ref[slot] = value

        copy_one(choice, [lambda ref=ref: ref[...] for ref in pool], write)


def reply(owner, pool, near, slots):
    whole = pl.BlockSpec(memory_space=pltpu.VMEM)
    scalar = pl.BlockSpec(memory_space=pltpu.SMEM)
    return pl.pallas_call(
        functools.partial(reply_kernel, near),
        in_specs=[scalar] + [whole] * len(pool),
        out_specs=whole,
        out_shape=jax.ShapeDtypeStruct((slots,) + pool[0].shape, bf16),
        compiler_params=pltpu.CompilerParams(vmem_limit_bytes=8 * MIB),
        name="reply",
    )(owner, *pool)


def lane_sum(array):
    halves = jnp.concatenate(pieces(array, 2), axis=1)
    return dot(halves, jnp.ones((2 * HD, HD), bf16))


def terms_kernel(capacity, count, parent_ref, decay_ref, queries_ref, keys_ref, values_ref, *refs):
    far = refs[:count]
    terms_ref, first_ref, second, parent_keys, parent_values = refs[count + 1 :]
    block = where_am_i()[1]
    steps, slots, per_block, columns = queries_ref.shape
    heads = columns // HD
    rows = steps * per_block
    lines = slots * rows
    halves = rows // (2 * capacity)
    split = columns // halves
    line = iota((lines, LANES), 0)
    near_col = jnp.full((lines, LANES), -1, jnp.int32)
    far_col = jnp.full((lines, LANES), -1, jnp.int32)
    sources = []
    for slot in range(slots):
        for beam in range(per_block):
            parent = parent_ref[slot, block * per_block + beam]
            source = lax.div(parent, per_block)
            rank = jnp.int32(0)
            for other in sources:
                rank = rank + jnp.where(other == source, 1, 0)
            sources.append(source)
            away = source ^ block
            near_at = slot * per_block + parent - source * per_block
            near_at = jnp.where(away == 0, near_at, -1)
            far_at = jnp.where(away == 0, -1, (away - 1) * rows + rank)
            here = line == slot * rows + per_block + beam
            near_col = jnp.where(here, near_at, near_col)
            far_col = jnp.where(here, far_at, far_col)
            own = block * per_block + beam
            now = slot * rows + beam
            then = now + per_block
            step_one = decay_ref[1, slot, pl.ds(own, 1), :]
            first_ref[now : now + 1, :] = decay_ref[0, slot, pl.ds(own, 1), :]
            first_ref[then : then + 1, :] = step_one + decay_ref[0, slot, pl.ds(parent, 1), :]
            second[now : now + 1, :] = jnp.full_like(step_one, -1e30)
            second[then : then + 1, :] = step_one
    first_ref[...] = jnp.exp(first_ref[...])
    second[...] = jnp.exp(second[...])
    held = slots * per_block
    own_hot = one_hot(iota((lines, held), 1) == near_col[:, :held])
    column = iota((lines, rows), 1)
    for half in range(halves):
        span = slice(half * split, (half + 1) * split)
        for kind, (ref, store) in enumerate(
            ((keys_ref, parent_keys), (values_ref, parent_values))
        ):
            own = stack_rows([ref[0, slot, :, span] for slot in range(slots)])
            picked = dot(own_hot, own.astype(bf16))
            for index, message in enumerate(far):
                low, high = half * 2 * capacity, kind * capacity
                hot = (column == far_col[:, :rows] - index * rows + low + high) & (
                    (far_col[:, :rows] >= index * rows)
                    & (far_col[:, :rows] < index * rows + capacity)
                )
                picked = picked + dot(one_hot(hot), message[:, columns:])
            store[:, span] = picked
    for head in range(heads):
        span = slice(head * HD, (head + 1) * HD)
        queries, keys, values = [
            stack_rows([ref[step, slot, :, span] for slot in range(slots) for step in range(steps)])
            for ref in (queries_ref, keys_ref, values_ref)
        ]
        own = lane_sum(queries * keys)
        parent = lane_sum(queries * parent_keys[:, span])
        terms_ref[:, span] = own * values + (
            second[:, head : head + 1] * parent
        ) * parent_values[:, span]


def step_terms(parents, decay, queries, keys, values, far, capacity, after):
    steps, slots, per_block, columns = queries.shape
    lines = steps * slots * per_block
    heads = columns // HD
    whole = pl.BlockSpec(memory_space=pltpu.VMEM)
    scalar = pl.BlockSpec(memory_space=pltpu.SMEM)
    return pl.pallas_call(
        functools.partial(terms_kernel, capacity, len(far)),
        in_specs=[scalar]
        + [whole] * (4 + len(far))
        + [pl.BlockSpec(memory_space=pl.ANY)],
        out_shape=[
            jax.ShapeDtypeStruct((lines, columns), f32),
            jax.ShapeDtypeStruct((lines, heads), f32),
        ],
        scratch_shapes=[
            pltpu.VMEM((lines, heads), f32),
            pltpu.VMEM((lines, columns), f32),
            pltpu.VMEM((lines, columns), f32),
        ],
        compiler_params=pltpu.CompilerParams(vmem_limit_bytes=12 * MIB),
        name="step_terms",
    )(parents, decay, queries, keys, values, *far, after)


def steps_kernel(heads, near, owner_ref, *refs):
    pool = refs[:-5]
    came_ref, terms_ref, first_ref, mixed_ref, sums_ref = refs[-5:]
    group, block = where_am_i()
    count = len(pool) // near
    slots, rows = came_ref.shape[:2]
    for slot, prompt in enumerate(prompts_of(owner_ref, group, slots)):
        offset = lax.div(prompt, count) ^ group
        choice = held_at(offset, near) * count + (lax.rem(prompt, count) ^ block)
        choice = jnp.where((offset & 1) != 0, len(pool), choice)
        lines = slice(slot * rows, (slot + 1) * rows)
        total = jnp.zeros((rows, HD), f32)
        for head in range(heads):
            span = slice(head * HD, (head + 1) * HD)
            read = came_ref[slot, :, span].astype(f32)
            for index in range(len(pool)):
                read = jnp.where(choice == index, pool[index][:, span].astype(f32), read)
            mixed = first_ref[lines, head : head + 1] * read + terms_ref[lines, span]
            mixed_ref[lines, span] = mixed
            total = total + mixed * mixed
        sums_ref[lines, :] = jnp.broadcast_to(
            jnp.sum(total, axis=1, keepdims=True), (rows, LANES)
        )


def steps_mix(owner, pool, near, came, terms, first):
    lines, columns = terms.shape
    whole = pl.BlockSpec(memory_space=pltpu.VMEM)
    scalar = pl.BlockSpec(memory_space=pltpu.SMEM)
    return pl.pallas_call(
        functools.partial(steps_kernel, columns // HD, near),
        in_specs=[scalar] + [whole] * (len(pool) + 3),
        out_shape=[
            jax.ShapeDtypeStruct((lines, columns), f32),
            jax.ShapeDtypeStruct((lines, LANES), f32),
        ],
        compiler_params=pltpu.CompilerParams(vmem_limit_bytes=12 * MIB),
        name="steps_mix",
    )(owner, *pool, came, terms, first)


def finish_kernel(width, count, gain_ref, mixed_ref, *refs):
    out_ref = refs[count]
    steps, slots, per_block, columns = out_ref.shape
    total = refs[0][...]
    for ref in refs[1:count]:
        total = total + ref[...]
    scale = lax.rsqrt(total * (1.0 / width) + epsilon)
    for column in range(0, columns, LANES):
        span = slice(column, column + LANES)
        scaled = (mixed_ref[:, span] * scale * gain_ref[:, span]).astype(bf16)
        for slot in range(slots):
            for step in range(steps):
                line = (slot * steps + step) * per_block
                out_ref[step, slot, :, span] = scaled[line : line + per_block]


def finish(gain, mixed, sums, shape):
    whole = pl.BlockSpec(memory_space=pltpu.VMEM)
    return pl.pallas_call(
        functools.partial(finish_kernel, HEAD_COUNT * HD, len(sums)),
        in_specs=[whole] * (2 + len(sums)),
        out_shape=jax.ShapeDtypeStruct(shape, bf16),
        compiler_params=pltpu.CompilerParams(vmem_limit_bytes=8 * MIB),
        name="finish",
    )(gain, mixed, *sums)


def swap(array, axis, bit):
    size = lax.axis_size(axis)
    return lax.ppermute(array, axis, [(index, index ^ bit) for index in range(size)])


def exchange(parts):
    order = sorted(range(1, len(parts)), key=lambda bit: (bit & 1, bit))
    came = {bit: swap(parts[bit], "dec", bit) for bit in order}
    return [came[bit] for bit in range(1, len(parts))]


def over_pre(array):
    size = lax.axis_size("pre")
    return [array] + [swap(array, "pre", bit) for bit in range(1, size)]


def local(
    prompt_queries,
    prompt_keys,
    prompt_values,
    prompt_decay,
    prompt_lengths,
    norm_gain,
    decode_owner,
    parent_beam,
    step_queries,
    step_keys,
    step_values,
    step_decay,
):
    tokens, columns = prompt_queries.shape[1:]
    slots = step_queries.shape[1]
    group_count, block_count = lax.axis_size("grp"), lax.axis_size("dec")
    near = group_count // 2
    capacity = (slots + block_count - 2) // (block_count - 1)
    gain = norm_gain[None]

    def widen(pool):
        bit = near
        while bit > 1:
            pool = pool + [swap(one, "grp", bit) for one in pool]
            bit //= 2
        return pool

    asked = widen([step_queries])
    sibling = swap(step_queries, "grp", 1)
    mixed, sums, state = prompt_pass(
        prompt_lengths, prompt_decay[0], prompt_queries[0], prompt_keys[0], prompt_values[0], sibling
    )
    far_rows, sums = lax.optimization_barrier((asked[1:], sums))
    asked = [step_queries] + far_rows + [sibling] + [swap(one, "grp", 1) for one in far_rows]

    messages = parcels(
        decode_owner, parent_beam, asked, step_keys, step_values, capacity, block_count
    )
    far = exchange(messages)
    squares = over_pre(sums)
    share = tokens // 8

    def norm(first, count, out, after, **more):
        return prompt_norm(
            prompt_lengths,
            gain,
            mixed,
            squares,
            first * share,
            count * share,
            out,
            after,
            **more,
        )

    prompt_out = norm(0, 2, None, messages[-1])
    state, prompt_out = lax.optimization_barrier((state, prompt_out))
    reads = read_states([messages[0]] + far, state)
    prompt_out = norm(2, 4, prompt_out, reads[-1], lines=2 * SUB)
    replies = exchange(reads)
    early = widen([reads[0]])
    replies, prompt_out = lax.optimization_barrier((replies, prompt_out))
    late = widen(replies)
    spread = len(early)
    pool = []
    for index in range(spread):
        pool = pool + [early[index]] + late[index * len(replies) : (index + 1) * len(replies)]
    terms, first = step_terms(
        parent_beam, step_decay, step_queries, step_keys, step_values, far, capacity, replies[-1]
    )
    pool, terms, prompt_out = lax.optimization_barrier((pool, terms, prompt_out))
    sent = reply(decode_owner, pool, near, slots)
    came = swap(sent, "grp", 1)
    step_mixed, step_sums = steps_mix(decode_owner, pool, near, came, terms, first)
    step_squares = over_pre(step_sums)
    prompt_out = norm(6, 2, prompt_out, step_sums, room=12)
    step_out = finish(gain, step_mixed, step_squares, step_queries.shape)
    return (prompt_out[None], step_out)


def solution(mesh):
    in_specs = (
        P(("grp", "dec"), None, "pre"),
        P(("grp", "dec"), None, "pre"),
        P(("grp", "dec"), None, "pre"),
        P(("grp", "dec"), "pre", None),
        P(("grp", "dec")),
        P("pre"),
        P(),
        P("grp", None),
        P(None, "grp", "dec", "pre"),
        P(None, "grp", "dec", "pre"),
        P(None, "grp", "dec", "pre"),
        P(None, "grp", None, "pre"),
    )
    out_specs = (P(("grp", "dec"), None, "pre"), P(None, "grp", "dec", "pre"))
    return jax.shard_map(local, mesh=mesh, in_specs=in_specs, out_specs=out_specs, check_vma=False)
```
